32 devices in a mesh: groups: 2 (over y), replica: 4 (over z), tensor: 4 (over x, core).
Axes of the slice: x: 2, y: 2, z: 4, core: 2. Of those that a mesh axis runs over, the one named last changes fastest.
Arguments:
- ssm_state: bfloat16 [64, 64, 64, 128], P(('groups', 'replica'), 'tensor'), parts along dimension 0, may hold values from -6 to 6
- conv_state: bfloat16 [64, 3, 4, 1280], P(('groups', 'replica'), None, 'tensor'), parts along dimension 0, may hold values from -6 to 6
- dst_replica: int32 [64], P(('groups', 'replica')), parts along dimension 0, may hold values from 0 to 3, as said below
- dst_slot: int32 [64], P(('groups', 'replica')), parts along dimension 0, may hold values from 0 to 7, as said below
- live: int32 [8], P('groups'), parts along dimension 0, may hold values from 1 to 8, as said below
- conv_in: bfloat16 [2, 64, 4, 1280], P(None, ('groups', 'replica'), 'tensor'), parts along dimension 1, may hold values from -6 to 6
- gate_in: bfloat16 [2, 64, 4096], P(None, ('groups', 'replica'), 'tensor'), parts along dimension 1, may hold values from -6 to 6
- dt_in: bfloat16 [2, 64, 64], P(None, ('groups', 'replica'), 'tensor'), parts along dimension 1, may hold values from -6 to 6
- conv_weight: bfloat16 [4, 4, 1280], P(None, 'tensor'), may hold values from -3 to 3
- conv_bias: bfloat16 [4, 1280], P('tensor'), may hold values from -3 to 3
- dt_bias: float32 [64], P('tensor'), may hold values from -4.6 to -2.3
- a_log: float32 [64], P('tensor'), may hold values from 0 to 2.77
- skip_gain: float32 [64], P('tensor'), may hold values from 0.5 to 2
- norm_gain: bfloat16 [4096], P('tensor'), may hold values from 0.099609375 to 1.8984375
- out_weight: bfloat16 [4096, 4096], P('tensor'), may hold values from -0.09375 to 0.09375
Outputs:
- mixed: bfloat16 [2, 64, 4096], P(None, ('groups', 'replica')), parts along dimension 1
- ssm_after: bfloat16 [64, 64, 64, 128], P(('groups', 'replica'), 'tensor'), parts along dimension 0
- conv_after: bfloat16 [64, 3, 4, 1280], P(('groups', 'replica'), None, 'tensor'), parts along dimension 0
The draws below stay inside these ranges and needn't reach their ends.
There are 2 independent parts, one for each index of `groups`. The reference program is written for one: setup_inputs(seed, part) draws one part's arguments, and reference() takes and returns one part's arrays. A program takes and returns all parts, laid end to end along the dimension named above; an argument that names none is the same for every part. Nothing has to cross between parts.
Inputs may be any that keep to these rules, and one draw needn't show every extreme that they name: `dst_replica`: the 8 requests of one replica go to 2 different replicas, exactly 4 to each; every replica receives exactly 8 requests. (dst_replica, dst_slot) differs between requests, so every slot of every replica receives one request. Some replica has all 8 slots live.
All inputs are finite; a program needn't handle non-finite values.
Results may differ from the reference program's by a relative error of at most 0.0049.
Values may be sent and summed in bfloat16 or wider, within the bound.
No kernel may reach another device: no remote copies, remote signals or barrier semaphores. Data moves between devices by JAX's collectives and lax.ppermute only.
A program may use at most 128 MiB of HBM per device.

```python
import math
import jax
import jax.numpy as jnp
from jax import lax

HEADS = 64
HEAD_DIM = 64
STATE = 128
GROUPS = 4
D = 4096
CONV = 4
STEPS = 2
SLOTS = 8
REPLICAS = 4
REQUESTS = 32
CAP = 4
INNER = 4096
CH_GROUP = 1280


def shuffled(one_key):
    return jax.random.permutation(one_key, SLOTS)


def migration_plan(key):
    group_total = SLOTS // CAP
    key_offset, key_target, key_order, key_slots = jax.random.split(key, 4)
    offsets = jax.random.permutation(key_offset, REPLICAS)[:group_total].astype(jnp.int32)
    targets = jax.random.permutation(key_target, REPLICAS).astype(jnp.int32)
    orders = jax.vmap(shuffled)(jax.random.split(key_order, REPLICAS)).astype(jnp.int32)
    group_of = orders // CAP
    member_of = orders % CAP
    senders = jnp.arange(REPLICAS, dtype=jnp.int32)[:, None]
    dest_replica = targets[(senders + offsets[group_of]) % REPLICAS]
    slot_orders = jax.vmap(shuffled)(jax.random.split(key_slots, REPLICAS)).astype(jnp.int32)
    dest_slot = slot_orders[dest_replica, group_of * CAP + member_of]
    return (dest_replica.reshape(REQUESTS).astype(jnp.int32), dest_slot.reshape(REQUESTS).astype(jnp.int32))


def draw_dst_replica(key, part):
    return migration_plan(key)[0]


def draw_dst_slot(key, part):
    return migration_plan(key)[1]


def draw_live(key, part):
    key = jax.random.fold_in(key, 11)
    first_key, second_key, full_key = jax.random.split(key, 3)
    first_draw = jax.random.randint(first_key, (REPLICAS,), 1, SLOTS + 1)
    second_draw = jax.random.randint(second_key, (REPLICAS,), 1, SLOTS + 1)
    counts = jnp.maximum(first_draw * second_draw // SLOTS, 1)
    busiest = jax.random.randint(full_key, (), 0, REPLICAS)
    return jnp.where(jnp.arange(REPLICAS) == busiest, SLOTS, counts).astype(jnp.int32)


def block_scale(own_key, shape, cuts, low, high):
    level = 1.0
    for position, blocks in cuts:
        draws = jax.random.uniform(jax.random.fold_in(jax.random.fold_in(own_key, 6), position), (blocks,), jnp.float32, low / len(cuts), high / len(cuts))
        level = level * jnp.repeat(jnp.exp(draws), shape[position] // blocks).reshape((-1,) + (1,) * (len(shape) - 1 - position))
    return level


def scatter_about(key, extent, spread, most, cuts=(), held_as=jnp.bfloat16):
    values = jax.random.normal(key, extent, jnp.float32) * spread
    if len(cuts) > 0:
        values = block_scale(key, extent, cuts, -0.22, 0.18) * values
    return jnp.clip(values, min=-most, max=most).astype(held_as)


def setup_inputs(seed: int = 0, part: int = 0) -> dict:
    splits = jax.random.split(jax.random.key(seed), 16)
    part_splits = jax.random.split(jax.random.fold_in(splits[15], part), 16)
    ssm_state = scatter_about(part_splits[0], (REQUESTS, HEADS, HEAD_DIM, STATE), 1.0, 6.0, ((0, 4), (1, 4)))
    conv_state = scatter_about(part_splits[1], (REQUESTS, CONV - 1, GROUPS, CH_GROUP), 1.0, 6.0, ((0, 4), (2, 4)))
    dst_replica = draw_dst_replica(jax.random.fold_in(jax.random.fold_in(splits[15], part), 71), part)
    dst_slot = draw_dst_slot(jax.random.fold_in(jax.random.fold_in(splits[15], part), 71), part)
    live = draw_live(jax.random.fold_in(jax.random.fold_in(splits[15], part), 71), part)
    conv_in = scatter_about(part_splits[5], (STEPS, REQUESTS, GROUPS, CH_GROUP), 1.0, 6.0, ((1, 4), (2, 4)))
    gate_in = scatter_about(part_splits[6], (STEPS, REQUESTS, INNER), 1.0, 6.0, ((1, 4), (2, 4)))
    dt_in = scatter_about(part_splits[7], (STEPS, REQUESTS, HEADS), 1.0, 6.0, ((1, 4), (2, 4)))
    conv_weight = scatter_about(splits[8], (CONV, GROUPS, CH_GROUP), CONV ** -0.5, 3.0, ((1, 4),))
    conv_bias = scatter_about(splits[9], (GROUPS, CH_GROUP), 0.5, 3.0, ((0, 4),))
    dt_bias = jnp.clip(-4.6 + 2.3 * jax.random.uniform(splits[10], (HEADS,), jnp.float32) ** block_scale(splits[10], (HEADS,), ((0, 4),), -0.2, 0.2), -4.6, -2.3)
    a_log = jnp.clip(2.77 * jax.random.uniform(splits[11], (HEADS,), jnp.float32) ** block_scale(splits[11], (HEADS,), ((0, 4),), -0.2, 0.2), 0.0, 2.77)
    skip_gain = jnp.clip(jnp.exp(math.log(2.0) - 1.3862944 * jax.random.uniform(splits[12], (HEADS,), jnp.float32) ** block_scale(splits[12], (HEADS,), ((0, 4),), -0.2, 0.2)), 0.5, 2.0)
    norm_gain = jnp.clip(1.0 + 0.18 * jax.random.normal(splits[13], (INNER,), jnp.float32), 0.099609375, 1.8984375).astype(jnp.bfloat16)
    out_weight = scatter_about(splits[14], (INNER, D), INNER ** -0.5, 0.09375, ((0, 4),))
    return dict(ssm_state=ssm_state, conv_state=conv_state, dst_replica=dst_replica, dst_slot=dst_slot, live=live, conv_in=conv_in, gate_in=gate_in, dt_in=dt_in, conv_weight=conv_weight, conv_bias=conv_bias, dt_bias=dt_bias, a_log=a_log, skip_gain=skip_gain, norm_gain=norm_gain, out_weight=out_weight)


def convolve(window_rows, conv_tokens, conv_weight, conv_bias):
    weight_rows = conv_weight.astype(jnp.float32)
    shift_rows = conv_bias.astype(jnp.float32)
    activations = []
    for step_index in range(conv_tokens.shape[0]):
        stacked = jnp.concatenate([window_rows, conv_tokens[step_index][:, None]], axis=1)
        summed = lax.optimization_barrier(jnp.sum(stacked.astype(jnp.float32) * weight_rows[None], axis=1)) + shift_rows
        activations.append(jax.nn.silu(summed))
        window_rows = stacked[:, 1:]
    return (activations, window_rows)

def advance(states_now, activations, dt_tokens, gate_tokens, dt_bias, a_log, skip_gain, norm_gain, heads_per_group):
    decay_rate = -jnp.exp(a_log)
    row_count, head_count, head_width, state_width = states_now.shape
    group_span = heads_per_group * head_width
    normed_list = []
    for step_index in range(len(activations)):
        act_rows = activations[step_index]
        group_count = act_rows.shape[1]
        values = act_rows[..., :group_span].reshape(row_count, head_count, head_width)
        input_map = jnp.repeat(act_rows[..., group_span:group_span + state_width], heads_per_group, axis=1)
        output_map = jnp.repeat(act_rows[..., group_span + state_width:], heads_per_group, axis=1)
        step_size = jax.nn.softplus(dt_tokens[step_index].astype(jnp.float32) + dt_bias)
        retained = jnp.exp(step_size * decay_rate)
        states_now = retained[:, :, None, None] * states_now + (step_size[:, :, None] * values)[:, :, :, None] * input_map[:, :, None, :]
        readout = jnp.einsum('shpn,shn->shp', states_now, output_map, precision=lax.Precision.HIGHEST) + skip_gain[None, :, None] * values
        gated_rows = readout.reshape(row_count, head_count * head_width) * jax.nn.silu(gate_tokens[step_index].astype(jnp.float32))
        grouped = gated_rows.reshape(row_count, group_count, group_span)
        factor = lax.rsqrt(lax.optimization_barrier(jnp.mean(grouped * grouped, axis=-1, keepdims=True)) + 1e-05)
        normed = (grouped * factor).reshape(row_count, head_count * head_width) * norm_gain.astype(jnp.float32)
        normed_list.append(normed.astype(jnp.bfloat16))
    return (jnp.stack(normed_list), states_now)

def reference(ssm_state, conv_state, dst_replica, dst_slot, live, conv_in, gate_in, dt_in, conv_weight, conv_bias, dt_bias, a_log, skip_gain, norm_gain, out_weight):
    target = (dst_replica * SLOTS + dst_slot).astype(jnp.int32)
    source = jnp.zeros((REQUESTS,), jnp.int32).at[target].set(jnp.arange(REQUESTS, dtype=jnp.int32))

    def one_block(block_index):
        first_row = (block_index * SLOTS).astype(jnp.int32)
        source_rows = lax.dynamic_slice_in_dim(source, first_row, SLOTS)
        states_now = jnp.take(ssm_state, source_rows, axis=0).astype(jnp.float32)
        windows_now = jnp.take(conv_state, source_rows, axis=0)
        conv_tokens = lax.dynamic_slice_in_dim(conv_in, first_row, SLOTS, 1)
        gate_tokens = lax.dynamic_slice_in_dim(gate_in, first_row, SLOTS, 1)
        dt_tokens = lax.dynamic_slice_in_dim(dt_in, first_row, SLOTS, 1)
        activations, windows_end = convolve(windows_now, conv_tokens, conv_weight, conv_bias)
        normed_all, states_end = advance(states_now, activations, dt_tokens, gate_tokens, dt_bias, a_log, skip_gain, norm_gain, HEADS // GROUPS)
        projected = jnp.dot(normed_all.reshape(STEPS * SLOTS, INNER), out_weight, preferred_element_type=jnp.float32).astype(jnp.bfloat16)
        live_rows = jnp.arange(SLOTS, dtype=jnp.int32) < live[block_index]
        mixed_block = jnp.where(live_rows[None, :, None], projected.reshape(STEPS, SLOTS, D), jnp.zeros((), jnp.bfloat16))
        ssm_block = jnp.where(live_rows[:, None, None, None], states_end.astype(jnp.bfloat16), jnp.zeros((), jnp.bfloat16))
        conv_block = jnp.where(live_rows[:, None, None, None], windows_end, jnp.zeros((), windows_end.dtype))
        return (mixed_block, ssm_block, conv_block)
    mixed_blocks, ssm_blocks, conv_blocks = lax.map(one_block, jnp.arange(REPLICAS, dtype=jnp.int32))
    mixed = jnp.transpose(mixed_blocks, (1, 0, 2, 3)).reshape(STEPS, REQUESTS, D)
    ssm_after = ssm_blocks.reshape(REQUESTS, HEADS, HEAD_DIM, STATE)
    conv_after = conv_blocks.reshape(REQUESTS, CONV - 1, GROUPS, CH_GROUP)
    return (mixed, ssm_after, conv_after)
```

```python
import functools
import itertools

import jax
import jax.numpy as jnp
from jax import lax
from jax.experimental import pallas as pl
from jax.experimental.pallas import tpu as pltpu
from jax.sharding import PartitionSpec as P

HEADS = 64
GROUPS = 4
BF16 = jnp.bfloat16
F32 = jnp.float32
SMEM = pltpu.SMEM
VMEM = pltpu.VMEM


def send_graphs(replicas):
    pairs = list(itertools.combinations(range(replicas), 2))
    graphs = []
    for chosen in itertools.product(pairs, repeat=replicas):
        if any(sum(d in pair for pair in chosen) != 2 for d in range(replicas)):
            continue
        for picks in itertools.product((0, 1), repeat=replicas):
            first = [chosen[s][picks[s]] for s in range(replicas)]
            if len(set(first)) == replicas:
                second = [chosen[s][1 - picks[s]] for s in range(replicas)]
                break
        code = sum(1 << (replicas * s + d) for s in range(replicas) for d in chosen[s])
        bits = sum(picks[s] << s for s in range(replicas))
        graphs.append((code, bits, first, second))
    return graphs


def route_kernel(graphs, replicas, slots, *refs):
    metas = refs[:replicas]
    states, windows, buf_a, buf_b, branch, arrival, win_rows, sems = refs[replicas:]
    half = slots // 2
    span = states.shape[1]
    taps = windows.shape[0]
    lanes = states.shape[2]
    block = win_rows.shape[1]
    me = lax.axis_index("replica")
    sources = [lax.rem(me + (replicas - k), replicas) for k in range(replicas)]
    code = jnp.int32(0)
    for k in range(replicas):
        edges = jnp.int32(0)
        for i in range(slots):
            edges = edges + jnp.left_shift(jnp.int32(1), metas[k][i])
        code = code + jnp.left_shift(lax.div(edges, jnp.int32(half)), sources[k] * replicas)
    index = jnp.int32(0)
    bits = jnp.int32(0)
    for j, (graph_code, graph_bits, _, _) in enumerate(graphs):
        hit = code == graph_code
        index = jnp.where(hit, j, index)
        bits = jnp.where(hit, graph_bits, bits)
    branch[0] = index

    def second_matching(source, target):
        row = lax.bitwise_and(
            lax.shift_right_logical(code, source * replicas), jnp.int32((1 << replicas) - 1)
        )
        below = lax.bitwise_and(row, jnp.left_shift(jnp.int32(1), target) - 1)
        rank = jnp.where(below != 0, 1, 0)
        pick = lax.bitwise_and(lax.shift_right_logical(bits, source), jnp.int32(1))
        return jnp.where(rank == pick, 0, 1)

    def pack(buf, place, i):
        rows = pl.ds(pl.multiple_of(place * span, span), span)
        return pltpu.make_async_copy(states.at[i], buf.at[rows], sems.at[i])

    counts = [jnp.int32(0), jnp.int32(0)]
    picked = []
    for i in range(slots):
        which = second_matching(me, metas[0][i])
        place = jnp.where(which == 0, counts[0], counts[1])
        counts = [counts[0] + (1 - which), counts[1] + which]
        picked.append((which, place))
        for m, buf in enumerate((buf_a, buf_b)):

            @pl.when(which == m)
            def _(buf=buf, i=i, place=place):
                pack(buf, place, i).start()

    for k in range(replicas):
        which = second_matching(sources[k], me)
        base = which * half + (2 * half if k == 0 else 0)
        count = jnp.int32(0)
        for i in range(slots):
            mine = metas[k][i] == me

            @pl.when(mine)
            def _(k=k, i=i, base=base, count=count):
                arrival[metas[k][slots + i]] = base + count

            count = count + jnp.where(mine, 1, 0)

    win_rows[...] = jnp.zeros_like(win_rows)
    for tap in range(taps):
        tokens = windows[tap].astype(F32)
        for i in range(slots):
            which, place = picked[i]
            win_rows[which, pl.ds(tap * half + place, 1), :] = tokens[i : i + 1]
    for m, buf in enumerate((buf_a, buf_b)):
        rows = win_rows[m].astype(BF16)
        for part in range(rows.shape[1] // lanes):
            top = half * span + part * block
            buf[top : top + block, :] = rows[:, part * lanes : (part + 1) * lanes]

    for i in range(slots):
        which, place = picked[i]
        for m, buf in enumerate((buf_a, buf_b)):

            @pl.when(which == m)
            def _(buf=buf, i=i, place=place):
                pack(buf, place, i).wait()


def parts_of(value, count):
    out = []
    for _ in range(count):
        part = value.astype(BF16).astype(F32)
        out.append(part)
        value = value - part
    return out


def sum_of_parts(rows, count):
    size = rows.shape[0] // count
    total = rows[:size]
    for part in range(1, count):
        total = total + rows[part * size : (part + 1) * size]
    return total


def silu(value):
    return value / (1.0 + jnp.exp(-value))


def softplus(value):
    return jnp.maximum(value, 0.0) + jnp.log1p(jnp.exp(-jnp.abs(value)))


def row_copy(arrival, sources, held, sems, row, act):
    slots, span, _ = held.shape
    half = slots // 2
    place = arrival[row]
    which = lax.div(place, half)
    rows = pl.ds(pl.multiple_of(lax.rem(place, half) * span, span), span)
    for m, source in enumerate(sources):

        @pl.when(which == m)
        def _(source=source):
            act(pltpu.make_async_copy(source.at[rows], held.at[row], sems.at[row]))


def mix_kernel(
    arrival,
    live,
    got_a,
    got_b,
    own_a,
    own_b,
    conv_in,
    gate_in,
    dt_in,
    conv_weight,
    conv_bias,
    dt_bias,
    a_log,
    skip_gain,
    norm_gain,
    out_weight,
    partial,
    updates,
    inputs,
    scale,
    last_window,
    held,
    weight_held,
    win_held,
    win_all,
    win_rows,
    in_sem,
    win_sem,
    weight_sem,
):
    slots, span, state = held.shape
    heads = dt_in.shape[2]
    half = slots // 2
    taps = win_rows.shape[0]
    chunk = out_weight.shape[0] // weight_sem.shape[0]
    sources = (got_a, got_b, own_a, own_b)
    win_size = win_held.shape[1]
    block = win_all.shape[1]

    def win_copy(m):
        return pltpu.make_async_copy(
            sources[m].at[pl.ds(half * span, win_size)], win_held.at[m], win_sem.at[m]
        )

    def weight_copy(part):
        rows = pl.ds(part * chunk, chunk)
        return pltpu.make_async_copy(
            out_weight.at[rows], weight_held.at[rows], weight_sem.at[part]
        )

    for m in range(len(sources)):
        win_copy(m).start()
    for row in range(slots):
        row_copy(arrival, sources, held, in_sem, row, lambda copy: copy.start())
    for part in range(weight_sem.shape[0]):
        weight_copy(part).start()

    steps, kept = [], []
    for step in range(2):
        steps.append(softplus(dt_in[step].astype(F32) + dt_bias[...]))
        kept.append(jnp.exp(steps[step] * -jnp.exp(a_log[...])))
    scale[...] = kept[0] * kept[1]
    per_head = jnp.concatenate(
        steps + kept + [jnp.broadcast_to(skip_gain[...], (slots, heads))], axis=0
    )
    head_of = lax.div(lax.broadcasted_iota(jnp.int32, (heads, span), 1), span // heads)
    spread = jnp.where(
        head_of == lax.broadcasted_iota(jnp.int32, (heads, span), 0), 1.0, 0.0
    ).astype(BF16)
    wide = sum_of_parts(
        jnp.dot(
            jnp.concatenate(parts_of(per_head, 3), axis=0).astype(BF16),
            spread,
            preferred_element_type=F32,
        ),
        3,
    )
    step_size = [wide[:slots], wide[slots : 2 * slots]]
    retained = [wide[2 * slots : 3 * slots], wide[3 * slots : 4 * slots]]
    skip = wide[4 * slots :]

    for m in range(len(sources)):
        win_copy(m).wait()
        for part in range(win_size // block):
            win_all[m, :, part * state : (part + 1) * state] = win_held[
                m, part * block : (part + 1) * block, :
            ].astype(F32)
    for row in range(slots):
        place = arrival[row]
        which = lax.div(place, half)
        member = lax.rem(place, half)
        for tap in range(taps):
            win_rows[tap, row : row + 1, :] = win_all[
                which, pl.ds(tap * half + member, 1), :
            ]
    last_window[...] = win_rows[taps - 1]

    line = [win_rows[tap] for tap in range(taps)] + [
        conv_in[0].astype(F32),
        conv_in[1].astype(F32),
    ]
    weights = conv_weight[...].astype(F32)
    acts = []
    for step in range(2):
        total = line[step] * weights[0:1]
        for tap in range(1, taps + 1):
            total = total + line[step + tap] * weights[tap : tap + 1]
        acts.append(silu(total + conv_bias[...].astype(F32)))
    xs = [act[:, :span] for act in acts]
    bs = [act[:, span : span + state] for act in acts]
    cs = [act[:, span + state :] for act in acts]
    us = [step_size[0] * xs[0], step_size[1] * xs[1]]
    updates[0] = retained[1] * us[0]
    updates[1] = us[1]
    inputs[0] = bs[0]
    inputs[1] = bs[1]
    queries = jnp.concatenate(parts_of(jnp.concatenate(cs, axis=0), 3), axis=0).astype(BF16)
    row_of = lax.rem(lax.broadcasted_iota(jnp.int32, (2 * slots, span), 0), slots)

    ys = jnp.zeros((2 * slots, span), F32)
    for row in range(slots):
        row_copy(arrival, sources, held, in_sem, row, lambda copy: copy.wait())
        got = lax.dot_general(
            queries, held[row], (((1,), (1,)), ((), ())), preferred_element_type=F32
        )
        ys = jnp.where(row_of == row, sum_of_parts(got, 3), ys)

    def dots(b, c):
        return jnp.sum(b * c, axis=1, keepdims=True)

    reads = [
        retained[0] * ys[:slots] + us[0] * dots(bs[0], cs[0]) + skip * xs[0],
        retained[1] * (retained[0] * ys[slots:] + us[0] * dots(bs[0], cs[1]))
        + us[1] * dots(bs[1], cs[1])
        + skip * xs[1],
    ]
    gains = norm_gain[...].astype(F32)
    normed = []
    for step in range(2):
        gated = reads[step] * silu(gate_in[step].astype(F32))
        factor = lax.rsqrt(jnp.sum(gated * gated, axis=1, keepdims=True) * (1.0 / span) + 1e-05)
        normed.append((gated * factor) * gains)
    normed = jnp.concatenate(normed, axis=0)
    alive = live[lax.axis_index("replica")]
    normed = jnp.where(row_of < alive, normed, 0.0).astype(BF16)
    total = None
    for part in range(weight_sem.shape[0]):
        weight_copy(part).wait()
        cut = slice(part * chunk, (part + 1) * chunk)
        term = jnp.dot(normed[:, cut], weight_held[cut, :], preferred_element_type=F32)
        total = term if total is None else total + term
    partial[...] = total.astype(BF16)


def state_kernel(
    arrival,
    live,
    got_a,
    got_b,
    own_a,
    own_b,
    updates,
    inputs,
    scale,
    last_window,
    conv_in,
    states_out,
    windows_out,
    held,
    held_out,
    in_sem,
    out_sem,
):
    slots, span, state = held.shape
    heads = scale.shape[1]
    width = span // heads
    sources = (got_a, got_b, own_a, own_b)
    for row in range(slots):
        row_copy(arrival, sources, held, in_sem, row, lambda copy: copy.start())
    alive = live[lax.axis_index("replica")]
    keep = lax.broadcasted_iota(jnp.int32, last_window.shape, 0) < alive
    for tap, tokens in enumerate(
        (last_window[...], conv_in[0].astype(F32), conv_in[1].astype(F32))
    ):
        windows_out[tap] = jnp.where(keep, tokens, 0.0).astype(BF16)

    u_parts, b_parts = [], []
    for step in range(2):
        u_hi, u_lo = parts_of(updates[step], 2)
        b_hi, b_lo = parts_of(inputs[step], 2)
        u_parts += [u_hi, u_hi, u_lo, u_lo]
        b_parts += [b_hi, b_lo, b_hi, b_lo]
    u_columns = jnp.transpose(jnp.concatenate(u_parts, axis=0)).astype(BF16)
    b_rows = jnp.concatenate(b_parts, axis=0)
    b_of = lax.rem(lax.broadcasted_iota(jnp.int32, b_rows.shape, 0), slots)
    for row in range(slots):
        row_copy(arrival, sources, held, in_sem, row, lambda copy: copy.wait())
        added = jnp.dot(
            u_columns,
            jnp.where(b_of == row, b_rows, 0.0).astype(BF16),
            preferred_element_type=F32,
        )
        for head in range(heads):
            rows = slice(head * width, (head + 1) * width)
            value = (
                scale[row : row + 1, head : head + 1] * held[row, rows, :].astype(F32)
                + added[rows]
            )
            held_out[row, rows, :] = jnp.where(row < alive, value, 0.0).astype(BF16)
        pltpu.make_async_copy(held_out.at[row], states_out.at[row], out_sem.at[row]).start()
    for row in range(slots):
        pltpu.make_async_copy(held_out.at[row], states_out.at[row], out_sem.at[row]).wait()


def routed(
    ssm_state,
    conv_state,
    dst_replica,
    dst_slot,
    live,
    conv_in,
    gate_in,
    dt_in,
    conv_weight,
    conv_bias,
    dt_bias,
    a_log,
    skip_gain,
    norm_gain,
    out_weight,
):
    replicas = lax.axis_size("replica")
    slots, heads, width, state = ssm_state.shape
    half = slots // 2
    span = heads * width
    taps, channels = conv_state.shape[1], conv_state.shape[3]
    columns = out_weight.shape[1]
    graphs = send_graphs(replicas)
    block = 16 * pl.cdiv(half * taps, 16)
    win_size = block * (channels // state)

    meta = jnp.concatenate([dst_replica, dst_slot])
    metas = [meta] + [
        lax.ppermute(meta, "replica", [(s, (s + k) % replicas) for s in range(replicas)])
        for k in range(1, replicas)
    ]
    tokens = conv_in.reshape(2, slots, channels)

    any_spec = pl.BlockSpec(memory_space=pl.ANY)
    smem = pl.BlockSpec(memory_space=SMEM)
    vmem = pl.BlockSpec(memory_space=VMEM)
    packed = jax.ShapeDtypeStruct((half * span + win_size, state), BF16)
    own_a, own_b, branch, arrival = pl.pallas_call(
        functools.partial(route_kernel, graphs, replicas, slots),
        out_shape=(
            packed,
            packed,
            jax.ShapeDtypeStruct((1,), jnp.int32),
            jax.ShapeDtypeStruct((slots,), jnp.int32),
        ),
        in_specs=[smem] * replicas + [any_spec, vmem],
        out_specs=(vmem, vmem, smem, smem),
        scratch_shapes=[VMEM((2, block, channels), F32), pltpu.SemaphoreType.DMA((slots,))],
        name="route",
    )(
        *metas,
        ssm_state.reshape(slots, span, state),
        jnp.swapaxes(conv_state, 0, 1).reshape(taps, slots, channels),
    )

    def along(first, second):
        def send(rows_a, rows_b):
            out = []
            for value, targets in ((rows_a, first), (rows_b, second)):
                moves = [(s, d) for s, d in enumerate(targets) if s != d]
                out.append(lax.ppermute(value, "replica", moves) if moves else value)
            return tuple(out)

        return send

    got_a, got_b = lax.switch(
        branch[0], [along(first, second) for _, _, first, second in graphs], own_a, own_b
    )
    arrived = (got_a, got_b, own_a, own_b)

    weight_parts = 4
    partial, updates, inputs, scale, last_window = pl.pallas_call(
        mix_kernel,
        out_shape=(
            jax.ShapeDtypeStruct((2 * slots, columns), BF16),
            jax.ShapeDtypeStruct((2, slots, span), F32),
            jax.ShapeDtypeStruct((2, slots, state), F32),
            jax.ShapeDtypeStruct((slots, heads), F32),
            jax.ShapeDtypeStruct((slots, channels), F32),
        ),
        in_specs=[smem, smem] + [any_spec] * 4 + [vmem] * 9 + [any_spec],
        out_specs=(vmem,) * 5,
        scratch_shapes=[
            VMEM((slots, span, state), BF16),
            VMEM(out_weight.shape, BF16),
            VMEM((4, win_size, state), BF16),
            VMEM((4, block, channels), F32),
            VMEM((taps, slots, channels), F32),
            pltpu.SemaphoreType.DMA((slots,)),
            pltpu.SemaphoreType.DMA((4,)),
            pltpu.SemaphoreType.DMA((weight_parts,)),
        ],
        compiler_params=pltpu.CompilerParams(vmem_limit_bytes=52 * 2**20),
        name="mix",
    )(
        arrival,
        live,
        *arrived,
        tokens,
        gate_in,
        dt_in,
        conv_weight.reshape(taps + 1, channels),
        conv_bias,
        dt_bias.reshape(1, heads),
        a_log.reshape(1, heads),
        skip_gain.reshape(1, heads),
        norm_gain.reshape(1, span),
        out_weight,
    )

    members = lax.axis_size("tensor")
    terms = [partial] + [
        lax.ppermute(partial, "tensor", [(i, i ^ k) for i in range(members)])
        for k in range(1, members)
    ]
    states_out, windows_out = pl.pallas_call(
        state_kernel,
        out_shape=(
            jax.ShapeDtypeStruct((slots, span, state), BF16),
            jax.ShapeDtypeStruct((taps, slots, channels), BF16),
        ),
        in_specs=[smem, smem] + [any_spec] * 4 + [vmem] * 5,
        out_specs=(any_spec, vmem),
        scratch_shapes=[
            VMEM((slots, span, state), BF16),
            VMEM((slots, span, state), BF16),
            pltpu.SemaphoreType.DMA((slots,)),
            pltpu.SemaphoreType.DMA((slots,)),
        ],
        compiler_params=pltpu.CompilerParams(vmem_limit_bytes=32 * 2**20),
        cost_estimate=pl.CostEstimate(
            flops=40 * slots * span * state,
            bytes_accessed=4 * slots * span * state,
            transcendentals=0,
        ),
        name="states",
    )(arrival, live, *arrived, updates, inputs, scale, last_window, tokens)

    terms = [term.astype(F32) for term in terms]
    while len(terms) > 1:
        terms = [terms[i] + terms[i + 1] for i in range(0, len(terms), 2)]
    mixed = terms[0].astype(BF16).reshape(2, slots, columns)
    conv_after = jnp.swapaxes(windows_out, 0, 1)[:, :, None, :]
    return mixed, states_out.reshape(ssm_state.shape), conv_after


def convolve(window_rows, conv_tokens, conv_weight, conv_bias):
    weight_rows = conv_weight.astype(jnp.float32)
    shift_rows = conv_bias.astype(jnp.float32)
    activations = []
    for step_index in range(conv_tokens.shape[0]):
        stacked = jnp.concatenate([window_rows, conv_tokens[step_index][:, None]], axis=1)
        summed = jnp.sum(stacked.astype(jnp.float32) * weight_rows[None], axis=1) + shift_rows
        activations.append(jax.nn.silu(summed))
        window_rows = stacked[:, 1:]
    return (activations, window_rows)


def advance(
    states_now,
    activations,
    dt_tokens,
    gate_tokens,
    dt_bias,
    a_log,
    skip_gain,
    norm_gain,
    heads_per_group,
):
    decay_rate = -jnp.exp(a_log)
    row_count, head_count, head_width, state_width = states_now.shape
    group_span = heads_per_group * head_width
    normed_list = []
    for step_index in range(len(activations)):
        act_rows = activations[step_index]
        group_count = act_rows.shape[1]
        values = act_rows[..., :group_span].reshape(row_count, head_count, head_width)
        input_map = jnp.repeat(
            act_rows[..., group_span : group_span + state_width], heads_per_group, axis=1
        )
        output_map = jnp.repeat(act_rows[..., group_span + state_width :], heads_per_group, axis=1)
        step_size = jax.nn.softplus(dt_tokens[step_index].astype(jnp.float32) + dt_bias)
        retained = jnp.exp(step_size * decay_rate)
        states_now = (
            retained[:, :, None, None] * states_now
            + (step_size[:, :, None] * values)[:, :, :, None] * input_map[:, :, None, :]
        )
        readout = (
            jnp.einsum("shpn,shn->shp", states_now, output_map, precision=lax.Precision.HIGHEST)
            + skip_gain[None, :, None] * values
        )
        gated_rows = readout.reshape(row_count, head_count * head_width) * jax.nn.silu(
            gate_tokens[step_index].astype(jnp.float32)
        )
        grouped = gated_rows.reshape(row_count, group_count, group_span)
        factor = lax.rsqrt(jnp.mean(grouped * grouped, axis=-1, keepdims=True) + 1e-05)
        normed = (grouped * factor).reshape(row_count, head_count * head_width) * norm_gain.astype(
            jnp.float32
        )
        normed_list.append(normed.astype(jnp.bfloat16))
    return (jnp.stack(normed_list), states_now)


def arrival_rows(received_ids, slot_count):
    wanted = jnp.arange(slot_count, dtype=jnp.int32)[:, None] == received_ids[None, :]
    buffer_index = jnp.arange(received_ids.shape[0], dtype=jnp.int32)
    return jnp.sum(jnp.where(wanted, buffer_index[None, :], 0), axis=1)


def padded(
    ssm_state,
    conv_state,
    dst_replica,
    dst_slot,
    live,
    conv_in,
    gate_in,
    dt_in,
    conv_weight,
    conv_bias,
    dt_bias,
    a_log,
    skip_gain,
    norm_gain,
    out_weight,
):
    replicas = lax.axis_size("replica")
    own_replica = lax.axis_index("replica")
    slot_count = ssm_state.shape[0]
    capacity = max(2, 2 * slot_count // replicas)
    row_index = jnp.arange(slot_count, dtype=jnp.int32)
    same_target = dst_replica[:, None] == dst_replica[None, :]
    earlier_rows = row_index[None, :] < row_index[:, None]
    member = jnp.sum(jnp.where(same_target & earlier_rows, 1, 0), axis=1).astype(jnp.int32)
    position = dst_replica * capacity + member
    buffer_rows = jnp.arange(replicas * capacity, dtype=jnp.int32)
    hit_table = position[None, :] == buffer_rows[:, None]
    picked = jnp.sum(jnp.where(hit_table, row_index[None, :], 0), axis=1)
    filled = jnp.any(hit_table, axis=1)
    send_ids = jnp.where(filled, jnp.take(dst_slot, picked), -1)
    send_windows = jnp.where(
        filled[:, None, None, None],
        jnp.take(conv_state, picked, axis=0),
        jnp.zeros((), conv_state.dtype),
    )
    send_states = jnp.where(
        filled[:, None, None, None],
        jnp.take(ssm_state, picked, axis=0),
        jnp.zeros((), ssm_state.dtype),
    )
    got_states, got_windows, got_ids = (
        lax.all_to_all(send_states, "replica", split_axis=0, concat_axis=0, tiled=True),
        lax.all_to_all(send_windows, "replica", split_axis=0, concat_axis=0, tiled=True),
        lax.all_to_all(send_ids, "replica", split_axis=0, concat_axis=0, tiled=True),
    )
    arrival = arrival_rows(got_ids, slot_count)
    windows_now = jnp.take(got_windows, arrival, axis=0)
    activations, windows_end = convolve(windows_now, conv_in, conv_weight, conv_bias)
    states_now = jnp.take(got_states, arrival, axis=0).astype(jnp.float32)
    normed_all, states_end = advance(
        states_now,
        activations,
        dt_in,
        gate_in,
        dt_bias,
        a_log,
        skip_gain,
        norm_gain,
        HEADS // GROUPS,
    )
    step_count = normed_all.shape[0]
    partial_value = jnp.dot(
        normed_all.reshape(step_count * slot_count, normed_all.shape[2]),
        out_weight,
        preferred_element_type=jnp.float32,
    )
    summed = lax.psum(partial_value, "tensor").astype(jnp.bfloat16)
    live_rows = row_index < live[own_replica]
    mixed = jnp.where(
        live_rows[None, :, None],
        summed.reshape(step_count, slot_count, summed.shape[1]),
        jnp.zeros((), jnp.bfloat16),
    )
    ssm_after = jnp.where(
        live_rows[:, None, None, None], states_end.astype(jnp.bfloat16), jnp.zeros((), jnp.bfloat16)
    )
    conv_after = jnp.where(
        live_rows[:, None, None, None], windows_end, jnp.zeros((), windows_end.dtype)
    )
    return (mixed, ssm_after, conv_after)


def solution(mesh):
    placed = (
        P(("groups", "replica"), "tensor", None, None),
        P(("groups", "replica"), None, "tensor", None),
        P(("groups", "replica")),
        P(("groups", "replica")),
        P("groups"),
        P(None, ("groups", "replica"), "tensor", None),
        P(None, ("groups", "replica"), "tensor"),
        P(None, ("groups", "replica"), "tensor"),
        P(None, "tensor", None),
        P("tensor", None),
        P("tensor"),
        P("tensor"),
        P("tensor"),
        P("tensor"),
        P("tensor", None),
    )
    shards = routed if mesh.shape["replica"] == 4 else padded
    return jax.shard_map(
        shards,
        mesh=mesh,
        in_specs=placed,
        out_specs=(
            P(None, ("groups", "replica"), None),
            P(("groups", "replica"), "tensor", None, None),
            P(("groups", "replica"), None, "tensor", None),
        ),
        check_vma=False,
    )
```

```python
import functools
import itertools

import jax
import jax.numpy as jnp
from jax import lax
from jax.experimental import pallas as pl
from jax.experimental.pallas import tpu as pltpu
from jax.sharding import PartitionSpec as P

HEADS = 64
GROUPS = 4
BF16 = jnp.bfloat16
F32 = jnp.float32
SMEM = pltpu.SMEM
VMEM = pltpu.VMEM


def send_graphs(replicas):
    pairs = list(itertools.combinations(range(replicas), 2))
    graphs = []
    for chosen in itertools.product(pairs, repeat=replicas):
        if any(sum(d in pair for pair in chosen) != 2 for d in range(replicas)):
            continue
        for picks in itertools.product((0, 1), repeat=replicas):
            first = [chosen[s][picks[s]] for s in range(replicas)]
            if len(set(first)) == replicas:
                second = [chosen[s][1 - picks[s]] for s in range(replicas)]
                break
        code = sum(1 << (replicas * s + d) for s in range(replicas) for d in chosen[s])
        bits = sum(picks[s] << s for s in range(replicas))
        graphs.append((code, bits, first, second))
    return graphs


def parts_of(value, count):
    out = []
    for _ in range(count):
        part = value.astype(BF16).astype(F32)
        out.append(part)
        value = value - part
    return out


def sum_of_parts(rows, count):
    size = rows.shape[0] // count
    total = rows[:size]
    for part in range(1, count):
        total = total + rows[part * size : (part + 1) * size]
    return total


def silu(value):
    return value / (1.0 + jnp.exp(-value))


def softplus(value):
    return jnp.maximum(value, 0.0) + jnp.log1p(jnp.exp(-jnp.abs(value)))


def prepare(small, wide, scale, gate, begun, gains):
    dt, tokens, gates, weights, bias, dt_shift, rates, skips, norms = small
    slots, heads = scale.shape
    span = wide.shape[1]
    steps, kept = [], []
    for step in range(2):
        steps.append(softplus(dt[step] + dt_shift))
        kept.append(jnp.exp(steps[step] * -jnp.exp(rates)))
    scale[...] = kept[0] * kept[1]
    per_head = jnp.concatenate(steps + kept + [jnp.broadcast_to(skips, (slots, heads))], axis=0)
    head_of = lax.div(lax.broadcasted_iota(jnp.int32, (heads, span), 1), span // heads)
    spread = jnp.where(
        head_of == lax.broadcasted_iota(jnp.int32, (heads, span), 0), 1.0, 0.0
    ).astype(BF16)
    wide[...] = sum_of_parts(
        jnp.dot(
            jnp.concatenate(parts_of(per_head, 3), axis=0).astype(BF16),
            spread,
            preferred_element_type=F32,
        ),
        3,
    )
    taps = weights.shape[0] - 1
    begun[0] = tokens[0] * weights[taps : taps + 1] + bias
    begun[1] = tokens[0] * weights[taps - 1 : taps] + tokens[1] * weights[taps : taps + 1] + bias
    for step in range(2):
        gate[step] = silu(gates[step])
    gains[...] = jnp.concatenate([norms[k : k + 1] for k in range(norms.shape[0])], axis=1)


def route_kernel(graphs, replicas, slots, *refs):
    to_replica, to_slot, *others = refs[: replicas + 1]
    states, *refs = refs[replicas + 1 :]
    count = (len(refs) - 3 - 9) // 2
    small, refs, held = refs[:count], refs[count:-count], refs[-count:]
    buf_a, buf_b, branch, loops, wide, scale, gate, begun, gains, win_rows, sems, small_sems = refs
    windows = held[0]
    fetches = [
        pltpu.make_async_copy(source, target, small_sems.at[k])
        for k, (source, target) in enumerate(zip(small, held))
    ]
    for fetch in fetches:
        fetch.start()
    half = slots // 2
    span = states.shape[1]
    taps = held[0].shape[0]
    lanes = states.shape[2]
    block = win_rows.shape[1]
    me = lax.axis_index("replica")
    sources = [lax.rem(me + (replicas - k), replicas) for k in range(replicas)]
    edges = jnp.int32(0)
    for i in range(slots):
        edges = edges + jnp.left_shift(jnp.int32(1), to_replica[i])
    code = jnp.left_shift(lax.div(edges, jnp.int32(half)), me * replicas)
    for k, other in enumerate(others, 1):
        flags = jnp.left_shift(jnp.int32(1), other[...]).astype(F32)
        edges = jnp.sum(flags).astype(jnp.int32)
        code = code + jnp.left_shift(lax.div(edges, jnp.int32(half)), sources[k] * replicas)
    index = jnp.int32(0)
    bits = jnp.int32(0)
    for j, (graph_code, graph_bits, _, _) in enumerate(graphs):
        hit = code == graph_code
        index = jnp.where(hit, j, index)
        bits = jnp.where(hit, graph_bits, bits)
    branch[0] = index

    def second_matching(source, target):
        row = lax.bitwise_and(
            lax.shift_right_logical(code, source * replicas), jnp.int32((1 << replicas) - 1)
        )
        below = lax.bitwise_and(row, jnp.left_shift(jnp.int32(1), target) - 1)
        rank = jnp.where(below != 0, 1, 0)
        pick = lax.bitwise_and(lax.shift_right_logical(bits, source), jnp.int32(1))
        return jnp.where(rank == pick, 0, 1)

    def pack(buf, place, i):
        rows = pl.ds(pl.multiple_of(place * span, span), span)
        return pltpu.make_async_copy(states.at[i], buf.at[rows], sems.at[i])

    counts = [jnp.int32(0), jnp.int32(0)]
    picked = []
    for i in range(slots):
        which = second_matching(me, to_replica[i])
        place = jnp.where(which == 0, counts[0], counts[1])
        counts = [counts[0] + (1 - which), counts[1] + which]
        picked.append((which, place))
        for m, buf in enumerate((buf_a, buf_b)):

            @pl.when(which == m)
            def _(buf=buf, i=i, place=place):
                pack(buf, place, i).start()

    loop = lax.bitwise_and(lax.shift_right_logical(code, me * replicas + me), jnp.int32(1))
    second = second_matching(me, me)
    loops[0] = loop * (1 - second)
    loops[1] = loop * second

    win_rows[...] = jnp.zeros_like(win_rows)
    for fetch in fetches:
        fetch.wait()
    for tap in range(taps):
        tokens = windows[tap].astype(F32)
        for i in range(slots):
            which, place = picked[i]
            win_rows[which, pl.ds(tap * half + place, 1), :] = tokens[i : i + 1]
    for i in range(slots):
        which, place = picked[i]
        win_rows[which, pl.ds(taps * half + place, 1), :] = jnp.full(
            (1, win_rows.shape[2]), to_slot[i].astype(F32)
        )
    for m, buf in enumerate((buf_a, buf_b)):
        rows = win_rows[m].astype(BF16)
        for part in range(rows.shape[1] // lanes):
            top = half * span + part * block
            buf[top : top + block, :] = rows[:, part * lanes : (part + 1) * lanes]

    prepare([ref[...].astype(F32) for ref in held[1:]], wide, scale, gate, begun, gains)

    for i in range(slots):
        pack(buf_a, 0, i).wait()


def fetch_rows(loops, pairs, held, sems):
    _, span, _ = held.shape
    half = held.shape[0] // 2
    for m, sources in enumerate(pairs):
        for own, source in enumerate(sources):

            @pl.when(loops[m] == own)
            def _(m=m, source=source):
                for member in range(half):
                    row = m * half + member
                    pltpu.make_async_copy(
                        source.at[pl.ds(member * span, span)], held.at[row], sems.at[row]
                    ).start()


def row_wait(pairs, held, sems, row):
    rows = pl.ds(0, held.shape[1])
    pltpu.make_async_copy(pairs[0][0].at[rows], held.at[row], sems.at[row]).wait()


def mix_kernel(
    loops,
    live,
    got_a,
    got_b,
    own_a,
    own_b,
    wide,
    gate,
    begun,
    conv_weight,
    norm_gain,
    out_weight,
    partial,
    updates,
    inputs,
    last_window,
    order,
    held,
    win_held,
    weight_held,
    in_sem,
    win_sem,
    weight_sem,
):
    slots, span, state = held.shape
    half = slots // 2
    taps = conv_weight.shape[0] - 1
    pairs = ((got_a, own_a), (got_b, own_b))
    win_size = win_held.shape[1]
    block = win_size // (begun.shape[2] // state)

    for m, sources in enumerate(pairs):
        for own, source in enumerate(sources):

            @pl.when(loops[m] == own)
            def _(m=m, source=source):
                pltpu.make_async_copy(
                    source.at[pl.ds(half * span, win_size)], win_held.at[m], win_sem.at[m]
                ).start()

    fetch_rows(loops, pairs, held, in_sem)
    chunk = out_weight.shape[0] // weight_sem.shape[0]
    fetches = []
    for part in range(weight_sem.shape[0]):
        rows = pl.ds(part * chunk, chunk)
        fetches.append(
            pltpu.make_async_copy(out_weight.at[rows], weight_held.at[rows], weight_sem.at[part])
        )
        fetches[part].start(priority=1)

    for m in range(len(pairs)):
        pltpu.make_async_copy(
            got_a.at[pl.ds(half * span, win_size)], win_held.at[m], win_sem.at[m]
        ).wait()
    parts = []
    for part in range(win_size // block):
        cut = slice(part * block, (part + 1) * block)
        parts.append(jnp.concatenate([win_held[m, cut, :] for m in range(len(pairs))], axis=0))
    top = taps * half
    arrived = [parts[0][m * block + top : m * block + top + half].astype(F32) for m in range(len(pairs))]
    order[...] = jnp.concatenate(arrived, axis=0)
    shape = (len(pairs) * block, taps * slots)
    column = lax.broadcasted_iota(jnp.int32, shape, 1)
    tap_of = lax.div(lax.rem(lax.broadcasted_iota(jnp.int32, shape, 0), block), half)
    slot_at = jnp.concatenate(
        [rows[:, : taps * slots] for rows in arrived for _ in range(block // half)], axis=0
    )
    choose = jnp.where(
        (tap_of == lax.div(column, slots)) & (slot_at == lax.rem(column, slots).astype(F32)),
        1.0,
        0.0,
    ).astype(BF16)
    windows = lax.dot_general(
        choose,
        jnp.concatenate(parts, axis=1),
        (((0,), (0,)), ((), ())),
        preferred_element_type=F32,
    )
    line = [windows[tap * slots : (tap + 1) * slots] for tap in range(taps)]
    last_window[...] = line[taps - 1]

    weights = conv_weight[...].astype(F32)
    acts = []
    for step in range(2):
        total = begun[step]
        for tap in range(taps - step):
            total = total + line[step + tap] * weights[tap : tap + 1]
        acts.append(silu(total))
    xs = [act[:, :span] for act in acts]
    bs = [act[:, span : span + state] for act in acts]
    cs = [act[:, span + state :] for act in acts]
    step_size = [wide[:slots], wide[slots : 2 * slots]]
    retained = [wide[2 * slots : 3 * slots], wide[3 * slots : 4 * slots]]
    skip = wide[4 * slots :]
    us = [step_size[0] * xs[0], step_size[1] * xs[1]]
    updates[0] = retained[1] * us[0]
    updates[1] = us[1]
    inputs[0] = bs[0]
    inputs[1] = bs[1]
    queries = jnp.concatenate(parts_of(jnp.concatenate(cs, axis=0), 3), axis=0).astype(BF16)
    row_of = lax.rem(lax.broadcasted_iota(jnp.int32, (2 * slots, span), 0), slots).astype(F32)
    slot_of = jnp.concatenate(arrived, axis=0)[:, :1]

    ys = jnp.zeros((2 * slots, span), F32)
    for row in range(slots):
        if row % (slots // 2) == 0:
            for later in range(row, row + (slots // 2)):
                row_wait(pairs, held, in_sem, later)
        got = lax.dot_general(
            queries, held[row], (((1,), (1,)), ((), ())), preferred_element_type=F32
        )
        ys = jnp.where(row_of == slot_of[row : row + 1], sum_of_parts(got, 3), ys)

    def dots(b, c):
        return jnp.sum(b * c, axis=1, keepdims=True)

    reads = [
        retained[0] * ys[:slots] + us[0] * dots(bs[0], cs[0]) + skip * xs[0],
        retained[1] * (retained[0] * ys[slots:] + us[0] * dots(bs[0], cs[1]))
        + us[1] * dots(bs[1], cs[1])
        + skip * xs[1],
    ]
    gains = norm_gain[...]
    normed = []
    for step in range(2):
        gated = reads[step] * gate[step]
        factor = lax.rsqrt(jnp.sum(gated * gated, axis=1, keepdims=True) * (1.0 / span) + 1e-05)
        normed.append((gated * factor) * gains)
    normed = jnp.concatenate(normed, axis=0)
    alive = live[lax.axis_index("replica")].astype(F32)
    normed = jnp.where(row_of < alive, normed, 0.0).astype(BF16)
    total = None
    for part, fetch in enumerate(fetches):
        fetch.wait()
        cut = slice(part * chunk, (part + 1) * chunk)
        term = jnp.dot(normed[:, cut], weight_held[cut, :], preferred_element_type=F32)
        total = term if total is None else total + term
    partial[...] = total.astype(BF16)


def state_kernel(
    loops,
    live,
    got_a,
    got_b,
    own_a,
    own_b,
    updates,
    inputs,
    scale,
    last_window,
    order,
    conv_in,
    states_out,
    windows_out,
    held,
    held_out,
    in_sem,
    out_sem,
):
    slots, span, state = held.shape
    heads = scale.shape[1]
    width = span // heads
    pairs = ((got_a, own_a), (got_b, own_b))
    fetch_rows(loops, pairs, held, in_sem)
    slot_of = [jnp.max(order[row : row + 1, :]).astype(jnp.int32) for row in range(slots)]
    alive = live[lax.axis_index("replica")]
    keep = lax.broadcasted_iota(jnp.int32, last_window.shape, 0) < alive
    for tap, tokens in enumerate(
        (last_window[...], conv_in[0].astype(F32), conv_in[1].astype(F32))
    ):
        windows_out[tap] = jnp.where(keep, tokens, 0.0).astype(BF16)

    u_parts, b_parts = [], []
    for step in range(2):
        u_hi, u_lo = parts_of(updates[step], 2)
        b_hi, b_lo = parts_of(inputs[step], 2)
        u_parts += [u_hi, u_hi, u_lo, u_lo]
        b_parts += [b_hi, b_lo, b_hi, b_lo]
    u_columns = jnp.transpose(jnp.concatenate(u_parts, axis=0)).astype(BF16)
    b_rows = jnp.concatenate(b_parts, axis=0)
    b_of = lax.rem(lax.broadcasted_iota(jnp.int32, b_rows.shape, 0), slots)
    for row in range(slots):
        slot = slot_of[row]
        factors = scale[pl.ds(slot, 1), :]
        if row % (slots // 2) == 0:
            for later in range(row, row + (slots // 2)):
                row_wait(pairs, held, in_sem, later)
        added = jnp.dot(
            u_columns,
            jnp.where(b_of == slot, b_rows, 0.0).astype(BF16),
            preferred_element_type=F32,
        )
        for head in range(heads):
            rows = slice(head * width, (head + 1) * width)
            value = (
                factors[:, head : head + 1] * held[row, rows, :].astype(F32)
                + added[rows]
            )
            held_out[row, rows, :] = jnp.where(slot < alive, value, 0.0).astype(BF16)
        pltpu.make_async_copy(held_out.at[row], states_out.at[slot], out_sem.at[row]).start()
    for row in range(slots):
        pltpu.make_async_copy(held_out.at[row], states_out.at[row], out_sem.at[row]).wait()


def routed(
    ssm_state,
    conv_state,
    dst_replica,
    dst_slot,
    live,
    conv_in,
    gate_in,
    dt_in,
    conv_weight,
    conv_bias,
    dt_bias,
    a_log,
    skip_gain,
    norm_gain,
    out_weight,
):
    replicas = lax.axis_size("replica")
    slots, heads, width, state = ssm_state.shape
    half = slots // 2
    span = heads * width
    taps, channels = conv_state.shape[1], conv_state.shape[3]
    columns = out_weight.shape[1]
    graphs = send_graphs(replicas)
    block = 16 * pl.cdiv(half * (taps + 1), 16)
    win_size = block * (channels // state)

    mine = dst_replica.reshape(1, slots)
    others = [
        lax.ppermute(mine, "replica", [(s, (s + k) % replicas) for s in range(replicas)])
        for k in range(1, replicas)
    ]
    tokens = conv_in.reshape(2, slots, channels)

    any_spec = pl.BlockSpec(memory_space=pl.ANY)
    smem = pl.BlockSpec(memory_space=SMEM)
    vmem = pl.BlockSpec(memory_space=VMEM)
    packed = jax.ShapeDtypeStruct((half * span + win_size, state), BF16)
    weights = conv_weight.reshape(taps + 1, channels)
    lanes = 128
    small = (
        jnp.swapaxes(conv_state, 0, 1).reshape(taps, slots, channels),
        dt_in,
        tokens,
        gate_in,
        weights,
        conv_bias,
        dt_bias.reshape(1, heads),
        a_log.reshape(1, heads),
        skip_gain.reshape(1, heads),
        norm_gain.reshape(span // lanes, lanes),
    )
    f32 = lambda *shape: jax.ShapeDtypeStruct(shape, F32)
    own_a, own_b, branch, loops, wide, scale, gate, begun, gains = pl.pallas_call(
        functools.partial(route_kernel, graphs, replicas, slots),
        out_shape=(
            packed,
            packed,
            jax.ShapeDtypeStruct((1,), jnp.int32),
            jax.ShapeDtypeStruct((2,), jnp.int32),
            f32(5 * slots, span),
            f32(slots, heads),
            f32(2, slots, span),
            f32(2, slots, channels),
            f32(1, span),
        ),
        in_specs=[smem] * 2 + [vmem] * (replicas - 1) + [any_spec] * (1 + len(small)),
        out_specs=(vmem, vmem, smem, smem) + (vmem,) * 5,
        scratch_shapes=[
            VMEM((2, block, channels), F32),
            pltpu.SemaphoreType.DMA((slots,)),
            pltpu.SemaphoreType.DMA((len(small),)),
        ]
        + [VMEM(value.shape, value.dtype) for value in small],
        name="route",
    )(dst_replica, dst_slot, *others, ssm_state.reshape(slots, span, state), *small)

    def along(first, second):
        def send(rows_a, rows_b):
            out = []
            for value, targets in ((rows_a, first), (rows_b, second)):
                moves = [(s, d) for s, d in enumerate(targets) if s != d]
                out.append(lax.ppermute(value, "replica", moves) if moves else value)
            return tuple(out)

        return send

    got_a, got_b = lax.switch(
        branch[0], [along(first, second) for _, _, first, second in graphs], own_a, own_b
    )
    arrived = (got_a, got_b, own_a, own_b)

    partial, updates, inputs, last_window, order = pl.pallas_call(
        mix_kernel,
        out_shape=(
            jax.ShapeDtypeStruct((2 * slots, columns), BF16),
            jax.ShapeDtypeStruct((2, slots, span), F32),
            jax.ShapeDtypeStruct((2, slots, state), F32),
            jax.ShapeDtypeStruct((slots, channels), F32),
            jax.ShapeDtypeStruct((slots, state), F32),
        ),
        in_specs=[smem, smem] + [any_spec] * 4 + [vmem] * 5 + [any_spec],
        out_specs=(vmem,) * 5,
        scratch_shapes=[
            VMEM((slots, span, state), BF16),
            VMEM((2, win_size, state), BF16),
            VMEM(out_weight.shape, BF16),
            pltpu.SemaphoreType.DMA((slots,)),
            pltpu.SemaphoreType.DMA((2,)),
            pltpu.SemaphoreType.DMA((8,)),
        ],
        compiler_params=pltpu.CompilerParams(vmem_limit_bytes=52 * 2**20),
        name="mix",
    )(
        loops,
        live,
        *arrived,
        wide,
        gate,
        begun,
        weights,
        gains,
        out_weight,
    )

    members = lax.axis_size("tensor")
    terms = [partial] + [
        lax.ppermute(partial, "tensor", [(i, i ^ k) for i in range(members)])
        for k in range(1, members)
    ]
    states_out, windows_out = pl.pallas_call(
        state_kernel,
        out_shape=(
            jax.ShapeDtypeStruct((slots, span, state), BF16),
            jax.ShapeDtypeStruct((taps, slots, channels), BF16),
        ),
        in_specs=[smem, smem] + [any_spec] * 4 + [vmem] * 6,
        out_specs=(any_spec, vmem),
        scratch_shapes=[
            VMEM((slots, span, state), BF16),
            VMEM((slots, span, state), BF16),
            pltpu.SemaphoreType.DMA((slots,)),
            pltpu.SemaphoreType.DMA((slots,)),
        ],
        compiler_params=pltpu.CompilerParams(vmem_limit_bytes=52 * 2**20),
        cost_estimate=pl.CostEstimate(
            flops=40 * slots * span * state,
            bytes_accessed=4 * slots * span * state,
            transcendentals=0,
        ),
        name="states",
    )(loops, live, *arrived, updates, inputs, scale, last_window, order, tokens)

    terms = [term.astype(F32) for term in terms]
    while len(terms) > 1:
        terms = [terms[i] + terms[i + 1] for i in range(0, len(terms), 2)]
    mixed = terms[0].astype(BF16).reshape(2, slots, columns)
    conv_after = jnp.swapaxes(windows_out, 0, 1)[:, :, None, :]
    return mixed, states_out.reshape(ssm_state.shape), conv_after


def convolve(window_rows, conv_tokens, conv_weight, conv_bias):
    weight_rows = conv_weight.astype(jnp.float32)
    shift_rows = conv_bias.astype(jnp.float32)
    activations = []
    for step_index in range(conv_tokens.shape[0]):
        stacked = jnp.concatenate([window_rows, conv_tokens[step_index][:, None]], axis=1)
        summed = jnp.sum(stacked.astype(jnp.float32) * weight_rows[None], axis=1) + shift_rows
        activations.append(jax.nn.silu(summed))
        window_rows = stacked[:, 1:]
    return (activations, window_rows)


def advance(
    states_now,
    activations,
    dt_tokens,
    gate_tokens,
    dt_bias,
    a_log,
    skip_gain,
    norm_gain,
    heads_per_group,
):
    decay_rate = -jnp.exp(a_log)
    row_count, head_count, head_width, state_width = states_now.shape
    group_span = heads_per_group * head_width
    normed_list = []
    for step_index in range(len(activations)):
        act_rows = activations[step_index]
        group_count = act_rows.shape[1]
        values = act_rows[..., :group_span].reshape(row_count, head_count, head_width)
        input_map = jnp.repeat(
            act_rows[..., group_span : group_span + state_width], heads_per_group, axis=1
        )
        output_map = jnp.repeat(act_rows[..., group_span + state_width :], heads_per_group, axis=1)
        step_size = jax.nn.softplus(dt_tokens[step_index].astype(jnp.float32) + dt_bias)
        retained = jnp.exp(step_size * decay_rate)
        states_now = (
            retained[:, :, None, None] * states_now
            + (step_size[:, :, None] * values)[:, :, :, None] * input_map[:, :, None, :]
        )
        readout = (
            jnp.einsum("shpn,shn->shp", states_now, output_map, precision=lax.Precision.HIGHEST)
            + skip_gain[None, :, None] * values
        )
        gated_rows = readout.reshape(row_count, head_count * head_width) * jax.nn.silu(
            gate_tokens[step_index].astype(jnp.float32)
        )
        grouped = gated_rows.reshape(row_count, group_count, group_span)
        factor = lax.rsqrt(jnp.mean(grouped * grouped, axis=-1, keepdims=True) + 1e-05)
        normed = (grouped * factor).reshape(row_count, head_count * head_width) * norm_gain.astype(
            jnp.float32
        )
        normed_list.append(normed.astype(jnp.bfloat16))
    return (jnp.stack(normed_list), states_now)


def arrival_rows(received_ids, slot_count):
    wanted = jnp.arange(slot_count, dtype=jnp.int32)[:, None] == received_ids[None, :]
    buffer_index = jnp.arange(received_ids.shape[0], dtype=jnp.int32)
    return jnp.sum(jnp.where(wanted, buffer_index[None, :], 0), axis=1)


def padded(
    ssm_state,
    conv_state,
    dst_replica,
    dst_slot,
    live,
    conv_in,
    gate_in,
    dt_in,
    conv_weight,
    conv_bias,
    dt_bias,
    a_log,
    skip_gain,
    norm_gain,
    out_weight,
):
    replicas = lax.axis_size("replica")
    own_replica = lax.axis_index("replica")
    slot_count = ssm_state.shape[0]
    capacity = max(2, 2 * slot_count // replicas)
    row_index = jnp.arange(slot_count, dtype=jnp.int32)
    same_target = dst_replica[:, None] == dst_replica[None, :]
    earlier_rows = row_index[None, :] < row_index[:, None]
    member = jnp.sum(jnp.where(same_target & earlier_rows, 1, 0), axis=1).astype(jnp.int32)
    position = dst_replica * capacity + member
    buffer_rows = jnp.arange(replicas * capacity, dtype=jnp.int32)
    hit_table = position[None, :] == buffer_rows[:, None]
    picked = jnp.sum(jnp.where(hit_table, row_index[None, :], 0), axis=1)
    filled = jnp.any(hit_table, axis=1)
    send_ids = jnp.where(filled, jnp.take(dst_slot, picked), -1)
    send_windows = jnp.where(
        filled[:, None, None, None],
        jnp.take(conv_state, picked, axis=0),
        jnp.zeros((), conv_state.dtype),
    )
    send_states = jnp.where(
        filled[:, None, None, None],
        jnp.take(ssm_state, picked, axis=0),
        jnp.zeros((), ssm_state.dtype),
    )
    got_states, got_windows, got_ids = (
        lax.all_to_all(send_states, "replica", split_axis=0, concat_axis=0, tiled=True),
        lax.all_to_all(send_windows, "replica", split_axis=0, concat_axis=0, tiled=True),
        lax.all_to_all(send_ids, "replica", split_axis=0, concat_axis=0, tiled=True),
    )
    arrival = arrival_rows(got_ids, slot_count)
    windows_now = jnp.take(got_windows, arrival, axis=0)
    activations, windows_end = convolve(windows_now, conv_in, conv_weight, conv_bias)
    states_now = jnp.take(got_states, arrival, axis=0).astype(jnp.float32)
    normed_all, states_end = advance(
        states_now,
        activations,
        dt_in,
        gate_in,
        dt_bias,
        a_log,
        skip_gain,
        norm_gain,
        HEADS // GROUPS,
    )
    step_count = normed_all.shape[0]
    partial_value = jnp.dot(
        normed_all.reshape(step_count * slot_count, normed_all.shape[2]),
        out_weight,
        preferred_element_type=jnp.float32,
    )
    summed = lax.psum(partial_value, "tensor").astype(jnp.bfloat16)
    live_rows = row_index < live[own_replica]
    mixed = jnp.where(
        live_rows[None, :, None],
        summed.reshape(step_count, slot_count, summed.shape[1]),
        jnp.zeros((), jnp.bfloat16),
    )
    ssm_after = jnp.where(
        live_rows[:, None, None, None], states_end.astype(jnp.bfloat16), jnp.zeros((), jnp.bfloat16)
    )
    conv_after = jnp.where(
        live_rows[:, None, None, None], windows_end, jnp.zeros((), windows_end.dtype)
    )
    return (mixed, ssm_after, conv_after)


def solution(mesh):
    placed = (
        P(("groups", "replica"), "tensor", None, None),
        P(("groups", "replica"), None, "tensor", None),
        P(("groups", "replica")),
        P(("groups", "replica")),
        P("groups"),
        P(None, ("groups", "replica"), "tensor", None),
        P(None, ("groups", "replica"), "tensor"),
        P(None, ("groups", "replica"), "tensor"),
        P(None, "tensor", None),
        P("tensor", None),
        P("tensor"),
        P("tensor"),
        P("tensor"),
        P("tensor"),
        P("tensor", None),
    )
    shards = routed if mesh.shape["replica"] == 4 else padded
    return jax.shard_map(
        shards,
        mesh=mesh,
        in_specs=placed,
        out_specs=(
            P(None, ("groups", "replica"), None),
            P(("groups", "replica"), "tensor", None, None),
            P(("groups", "replica"), None, "tensor", None),
        ),
        check_vma=False,
    )
```

```python
import functools
import itertools

import jax
import jax.numpy as jnp
from jax import lax
from jax.experimental import pallas as pl
from jax.experimental.pallas import tpu as pltpu
from jax.sharding import PartitionSpec as P

HEADS = 64
GROUPS = 4
BF16 = jnp.bfloat16
F32 = jnp.float32
SMEM = pltpu.SMEM
VMEM = pltpu.VMEM


def send_graphs(replicas):
    pairs = list(itertools.combinations(range(replicas), 2))
    graphs = []
    for chosen in itertools.product(pairs, repeat=replicas):
        if any(sum(d in pair for pair in chosen) != 2 for d in range(replicas)):
            continue
        for picks in itertools.product((0, 1), repeat=replicas):
            first = [chosen[s][picks[s]] for s in range(replicas)]
            if len(set(first)) == replicas:
                second = [chosen[s][1 - picks[s]] for s in range(replicas)]
                break
        code = sum(1 << (replicas * s + d) for s in range(replicas) for d in chosen[s])
        bits = sum(picks[s] << s for s in range(replicas))
        graphs.append((code, bits, first, second))
    return graphs


def parts_of(value, count):
    out = []
    for _ in range(count):
        part = value.astype(BF16).astype(F32)
        out.append(part)
        value = value - part
    return out


def sum_of_parts(rows, count):
    size = rows.shape[0] // count
    total = rows[:size]
    for part in range(1, count):
        total = total + rows[part * size : (part + 1) * size]
    return total


def silu(value):
    return value / (1.0 + jnp.exp(-value))


def softplus(value):
    return jnp.maximum(value, 0.0) + jnp.log1p(jnp.exp(-jnp.abs(value)))


def prepare(small, wide, scale, gate, begun, gains):
    dt, tokens, gates, weights, bias, dt_shift, rates, skips, norms = small
    slots, heads = scale.shape
    span = wide.shape[1]
    steps, kept = [], []
    for step in range(2):
        steps.append(softplus(dt[step] + dt_shift))
        kept.append(jnp.exp(steps[step] * -jnp.exp(rates)))
    scale[...] = kept[0] * kept[1]
    per_head = jnp.concatenate(steps + kept + [jnp.broadcast_to(skips, (slots, heads))], axis=0)
    head_of = lax.div(lax.broadcasted_iota(jnp.int32, (heads, span), 1), span // heads)
    spread = jnp.where(
        head_of == lax.broadcasted_iota(jnp.int32, (heads, span), 0), 1.0, 0.0
    ).astype(BF16)
    wide[...] = sum_of_parts(
        jnp.dot(
            jnp.concatenate(parts_of(per_head, 3), axis=0).astype(BF16),
            spread,
            preferred_element_type=F32,
        ),
        3,
    )
    taps = weights.shape[0] - 1
    begun[0] = tokens[0] * weights[taps : taps + 1] + bias
    begun[1] = tokens[0] * weights[taps - 1 : taps] + tokens[1] * weights[taps : taps + 1] + bias
    for step in range(2):
        gate[step] = silu(gates[step])
    gains[...] = jnp.concatenate([norms[k : k + 1] for k in range(norms.shape[0])], axis=1)


def near_kernel(states_in, windows_in, states, windows, sems):
    copies = [
        pltpu.make_async_copy(states_in.at[row], states.at[row], sems.at[row])
        for row in range(states.shape[0])
    ]
    for copy in copies:
        copy.start()
    windows[...] = windows_in[...].astype(F32)
    for copy in copies:
        copy.wait()


def route_kernel(graphs, replicas, slots, *refs):
    to_replica, to_slot, *others = refs[: replicas + 1]
    states, windows, buf_a, buf_b, branch, loops, win_rows, sems = refs[replicas + 1 :]
    half = slots // 2
    span = states.shape[1]
    taps = windows.shape[0]
    lanes = states.shape[2]
    block = win_rows.shape[1]
    me = lax.axis_index("replica")
    sources = [lax.rem(me + (replicas - k), replicas) for k in range(replicas)]
    edges = jnp.int32(0)
    for i in range(slots):
        edges = edges + jnp.left_shift(jnp.int32(1), to_replica[i])
    code = jnp.left_shift(lax.div(edges, jnp.int32(half)), me * replicas)
    for k, other in enumerate(others, 1):
        flags = jnp.left_shift(jnp.int32(1), other[...]).astype(F32)
        edges = jnp.sum(flags).astype(jnp.int32)
        code = code + jnp.left_shift(lax.div(edges, jnp.int32(half)), sources[k] * replicas)
    index = jnp.int32(0)
    bits = jnp.int32(0)
    for j, (graph_code, graph_bits, _, _) in enumerate(graphs):
        hit = code == graph_code
        index = jnp.where(hit, j, index)
        bits = jnp.where(hit, graph_bits, bits)
    branch[0] = index

    def second_matching(source, target):
        row = lax.bitwise_and(
            lax.shift_right_logical(code, source * replicas), jnp.int32((1 << replicas) - 1)
        )
        below = lax.bitwise_and(row, jnp.left_shift(jnp.int32(1), target) - 1)
        rank = jnp.where(below != 0, 1, 0)
        pick = lax.bitwise_and(lax.shift_right_logical(bits, source), jnp.int32(1))
        return jnp.where(rank == pick, 0, 1)

    def pack(buf, place, i):
        rows = pl.ds(pl.multiple_of(place * span, span), span)
        return pltpu.make_async_copy(states.at[i], buf.at[rows], sems.at[i])

    counts = [jnp.int32(0), jnp.int32(0)]
    picked = []
    for i in range(slots):
        which = second_matching(me, to_replica[i])
        place = jnp.where(which == 0, counts[0], counts[1])
        counts = [counts[0] + (1 - which), counts[1] + which]
        picked.append((which, place))
        for m, buf in enumerate((buf_a, buf_b)):

            @pl.when(which == m)
            def _(buf=buf, i=i, place=place):
                pack(buf, place, i).start()

    loop = lax.bitwise_and(lax.shift_right_logical(code, me * replicas + me), jnp.int32(1))
    second = second_matching(me, me)
    loops[0] = loop * (1 - second)
    loops[1] = loop * second

    win_rows[...] = jnp.zeros_like(win_rows)
    for tap in range(taps):
        for i in range(slots):
            which, place = picked[i]
            win_rows[which, pl.ds(tap * half + place, 1), :] = windows[tap, i : i + 1, :]
    for i in range(slots):
        which, place = picked[i]
        win_rows[which, pl.ds(taps * half + place, 1), :] = jnp.full(
            (1, win_rows.shape[2]), to_slot[i].astype(F32)
        )
    for m, buf in enumerate((buf_a, buf_b)):
        rows = win_rows[m].astype(BF16)
        for part in range(rows.shape[1] // lanes):
            top = half * span + part * block
            buf[top : top + block, :] = rows[:, part * lanes : (part + 1) * lanes]

    for i in range(slots):
        pack(buf_a, 0, i).wait()


def fetch_rows(loops, pairs, held, sems):
    _, span, _ = held.shape
    half = held.shape[0] // 2
    for m, sources in enumerate(pairs):
        for own, source in enumerate(sources):

            @pl.when(loops[m] == own)
            def _(m=m, source=source):
                for member in range(half):
                    row = m * half + member
                    pltpu.make_async_copy(
                        source.at[pl.ds(member * span, span)], held.at[row], sems.at[row]
                    ).start()


def row_wait(pairs, held, sems, row):
    rows = pl.ds(0, held.shape[1])
    pltpu.make_async_copy(pairs[0][0].at[rows], held.at[row], sems.at[row]).wait()


def mix_kernel(
    loops,
    live,
    got_a,
    got_b,
    own_a,
    own_b,
    dt_in,
    conv_in,
    gate_in,
    conv_weight,
    conv_bias,
    dt_bias,
    a_log,
    skip_gain,
    norm_gain,
    out_weight,
    partial,
    updates,
    inputs,
    last_window,
    order,
    scale,
    held,
    win_held,
    weight_held,
    wide,
    gate,
    begun,
    gains,
    in_sem,
    win_sem,
    weight_sem,
):
    slots, span, state = held.shape
    half = slots // 2
    taps = conv_weight.shape[0] - 1
    pairs = ((got_a, own_a), (got_b, own_b))
    win_size = win_held.shape[1]
    block = win_size // (begun.shape[2] // state)

    for m, sources in enumerate(pairs):
        for own, source in enumerate(sources):

            @pl.when(loops[m] == own)
            def _(m=m, source=source):
                pltpu.make_async_copy(
                    source.at[pl.ds(half * span, win_size)], win_held.at[m], win_sem.at[m]
                ).start()

    fetch_rows(loops, pairs, held, in_sem)
    chunk = out_weight.shape[0] // weight_sem.shape[0]
    fetches = []
    for part in range(weight_sem.shape[0]):
        rows = pl.ds(part * chunk, chunk)
        fetches.append(
            pltpu.make_async_copy(out_weight.at[rows], weight_held.at[rows], weight_sem.at[part])
        )
        fetches[part].start(priority=1)

    small = (
        dt_in, conv_in, gate_in, conv_weight, conv_bias, dt_bias, a_log, skip_gain, norm_gain,
    )
    prepare([ref[...].astype(F32) for ref in small], wide, scale, gate, begun, gains)

    for m in range(len(pairs)):
        pltpu.make_async_copy(
            got_a.at[pl.ds(half * span, win_size)], win_held.at[m], win_sem.at[m]
        ).wait()
    parts = []
    for part in range(win_size // block):
        cut = slice(part * block, (part + 1) * block)
        parts.append(jnp.concatenate([win_held[m, cut, :] for m in range(len(pairs))], axis=0))
    top = taps * half
    arrived = [parts[0][m * block + top : m * block + top + half].astype(F32) for m in range(len(pairs))]
    order[...] = jnp.concatenate(arrived, axis=0)
    shape = (len(pairs) * block, taps * slots)
    column = lax.broadcasted_iota(jnp.int32, shape, 1)
    tap_of = lax.div(lax.rem(lax.broadcasted_iota(jnp.int32, shape, 0), block), half)
    slot_at = jnp.concatenate(
        [rows[:, : taps * slots] for rows in arrived for _ in range(block // half)], axis=0
    )
    choose = jnp.where(
        (tap_of == lax.div(column, slots)) & (slot_at == lax.rem(column, slots).astype(F32)),
        1.0,
        0.0,
    ).astype(BF16)
    windows = lax.dot_general(
        choose,
        jnp.concatenate(parts, axis=1),
        (((0,), (0,)), ((), ())),
        preferred_element_type=F32,
    )
    line = [windows[tap * slots : (tap + 1) * slots] for tap in range(taps)]
    last_window[...] = line[taps - 1]

    weights = conv_weight[...].astype(F32)
    acts = []
    for step in range(2):
        total = begun[step]
        for tap in range(taps - step):
            total = total + line[step + tap] * weights[tap : tap + 1]
        acts.append(silu(total))
    xs = [act[:, :span] for act in acts]
    bs = [act[:, span : span + state] for act in acts]
    cs = [act[:, span + state :] for act in acts]
    step_size = [wide[:slots], wide[slots : 2 * slots]]
    retained = [wide[2 * slots : 3 * slots], wide[3 * slots : 4 * slots]]
    skip = wide[4 * slots :]
    us = [step_size[0] * xs[0], step_size[1] * xs[1]]
    updates[0] = retained[1] * us[0]
    updates[1] = us[1]
    inputs[0] = bs[0]
    inputs[1] = bs[1]
    queries = jnp.concatenate(parts_of(jnp.concatenate(cs, axis=0), 3), axis=0).astype(BF16)
    row_of = lax.rem(lax.broadcasted_iota(jnp.int32, (2 * slots, span), 0), slots).astype(F32)
    slot_of = jnp.concatenate(arrived, axis=0)[:, :1]

    ys = jnp.zeros((2 * slots, span), F32)
    for row in range(slots):
        if row % (slots // 2) == 0:
            for later in range(row, row + (slots // 2)):
                row_wait(pairs, held, in_sem, later)
        got = lax.dot_general(
            queries, held[row], (((1,), (1,)), ((), ())), preferred_element_type=F32
        )
        ys = jnp.where(row_of == slot_of[row : row + 1], sum_of_parts(got, 3), ys)

    def dots(b, c):
        return jnp.sum(b * c, axis=1, keepdims=True)

    reads = [
        retained[0] * ys[:slots] + us[0] * dots(bs[0], cs[0]) + skip * xs[0],
        retained[1] * (retained[0] * ys[slots:] + us[0] * dots(bs[0], cs[1]))
        + us[1] * dots(bs[1], cs[1])
        + skip * xs[1],
    ]
    normed = []
    for step in range(2):
        gated = reads[step] * gate[step]
        factor = lax.rsqrt(jnp.sum(gated * gated, axis=1, keepdims=True) * (1.0 / span) + 1e-05)
        normed.append((gated * factor) * gains[...])
    normed = jnp.concatenate(normed, axis=0)
    alive = live[lax.axis_index("replica")].astype(F32)
    normed = jnp.where(row_of < alive, normed, 0.0).astype(BF16)
    total = None
    for part, fetch in enumerate(fetches):
        fetch.wait()
        cut = slice(part * chunk, (part + 1) * chunk)
        term = jnp.dot(normed[:, cut], weight_held[cut, :], preferred_element_type=F32)
        total = term if total is None else total + term
    partial[...] = total.astype(BF16)


def state_kernel(
    loops,
    live,
    got_a,
    got_b,
    own_a,
    own_b,
    updates,
    inputs,
    scale,
    last_window,
    order,
    conv_in,
    states_out,
    windows_out,
    held,
    held_out,
    in_sem,
    out_sem,
):
    slots, span, state = held.shape
    heads = scale.shape[1]
    width = span // heads
    pairs = ((got_a, own_a), (got_b, own_b))
    fetch_rows(loops, pairs, held, in_sem)
    slot_of = [jnp.max(order[row : row + 1, :]).astype(jnp.int32) for row in range(slots)]
    alive = live[lax.axis_index("replica")]
    keep = lax.broadcasted_iota(jnp.int32, last_window.shape, 0) < alive
    for tap, tokens in enumerate(
        (last_window[...], conv_in[0].astype(F32), conv_in[1].astype(F32))
    ):
        windows_out[tap] = jnp.where(keep, tokens, 0.0).astype(BF16)

    u_parts, b_parts = [], []
    for step in range(2):
        u_hi, u_lo = parts_of(updates[step], 2)
        b_hi, b_lo = parts_of(inputs[step], 2)
        u_parts += [u_hi, u_hi, u_lo, u_lo]
        b_parts += [b_hi, b_lo, b_hi, b_lo]
    u_columns = jnp.transpose(jnp.concatenate(u_parts, axis=0)).astype(BF16)
    b_rows = jnp.concatenate(b_parts, axis=0)
    b_of = lax.rem(lax.broadcasted_iota(jnp.int32, b_rows.shape, 0), slots)
    for row in range(slots):
        slot = slot_of[row]
        factors = scale[pl.ds(slot, 1), :]
        if row % (slots // 2) == 0:
            for later in range(row, row + (slots // 2)):
                row_wait(pairs, held, in_sem, later)
        added = jnp.dot(
            u_columns,
            jnp.where(b_of == slot, b_rows, 0.0).astype(BF16),
            preferred_element_type=F32,
        )
        for head in range(heads):
            rows = slice(head * width, (head + 1) * width)
            value = (
                factors[:, head : head + 1] * held[row, rows, :].astype(F32)
                + added[rows]
            )
            held_out[row, rows, :] = jnp.where(slot < alive, value, 0.0).astype(BF16)
        pltpu.make_async_copy(held_out.at[row], states_out.at[slot], out_sem.at[row]).start()
    for row in range(slots):
        pltpu.make_async_copy(held_out.at[row], states_out.at[row], out_sem.at[row]).wait()


def routed(
    ssm_state,
    conv_state,
    dst_replica,
    dst_slot,
    live,
    conv_in,
    gate_in,
    dt_in,
    conv_weight,
    conv_bias,
    dt_bias,
    a_log,
    skip_gain,
    norm_gain,
    out_weight,
):
    replicas = lax.axis_size("replica")
    slots, heads, width, state = ssm_state.shape
    half = slots // 2
    span = heads * width
    taps, channels = conv_state.shape[1], conv_state.shape[3]
    columns = out_weight.shape[1]
    graphs = send_graphs(replicas)
    block = 16 * pl.cdiv(half * (taps + 1), 16)
    win_size = block * (channels // state)

    mine = dst_replica.reshape(1, slots)
    others = [
        lax.ppermute(mine, "replica", [(s, (s + k) % replicas) for s in range(replicas)])
        for k in range(1, replicas)
    ]
    tokens = conv_in.reshape(2, slots, channels)

    any_spec = pl.BlockSpec(memory_space=pl.ANY)
    smem = pl.BlockSpec(memory_space=SMEM)
    vmem = pl.BlockSpec(memory_space=VMEM)
    packed = jax.ShapeDtypeStruct((half * span + win_size, state), BF16)
    weights = conv_weight.reshape(taps + 1, channels)
    lanes = 128
    small = (
        dt_in,
        tokens,
        gate_in,
        weights,
        conv_bias,
        dt_bias.reshape(1, heads),
        a_log.reshape(1, heads),
        skip_gain.reshape(1, heads),
        norm_gain.reshape(span // lanes, lanes),
    )
    f32 = lambda *shape: jax.ShapeDtypeStruct(shape, F32)
    states, windows = pl.pallas_call(
        near_kernel,
        out_shape=(
            jax.ShapeDtypeStruct((slots, span, state), BF16),
            f32(taps, slots, channels),
        ),
        in_specs=[any_spec, vmem],
        out_specs=(vmem, vmem),
        scratch_shapes=[pltpu.SemaphoreType.DMA((slots,))],
        compiler_params=pltpu.CompilerParams(vmem_limit_bytes=16 * 2**20),
        name="near",
    )(
        ssm_state.reshape(slots, span, state),
        jnp.swapaxes(conv_state, 0, 1).reshape(taps, slots, channels),
    )

    own_a, own_b, branch, loops = pl.pallas_call(
        functools.partial(route_kernel, graphs, replicas, slots),
        out_shape=(
            packed,
            packed,
            jax.ShapeDtypeStruct((1,), jnp.int32),
            jax.ShapeDtypeStruct((2,), jnp.int32),
        ),
        in_specs=[smem] * 2 + [vmem] * (replicas + 1),
        out_specs=(vmem, vmem, smem, smem),
        scratch_shapes=[VMEM((2, block, channels), F32), pltpu.SemaphoreType.DMA((slots,))],
        compiler_params=pltpu.CompilerParams(vmem_limit_bytes=16 * 2**20),
        name="route",
    )(dst_replica, dst_slot, *others, states, windows)

    def along(first, second):
        def send(rows_a, rows_b):
            out = []
            for value, targets in ((rows_a, first), (rows_b, second)):
                moves = [(s, d) for s, d in enumerate(targets) if s != d]
                out.append(lax.ppermute(value, "replica", moves) if moves else value)
            return tuple(out)

        return send

    got_a, got_b = lax.switch(
        branch[0], [along(first, second) for _, _, first, second in graphs], own_a, own_b
    )
    arrived = (got_a, got_b, own_a, own_b)

    partial, updates, inputs, last_window, order, scale = pl.pallas_call(
        mix_kernel,
        out_shape=(
            jax.ShapeDtypeStruct((2 * slots, columns), BF16),
            jax.ShapeDtypeStruct((2, slots, span), F32),
            jax.ShapeDtypeStruct((2, slots, state), F32),
            jax.ShapeDtypeStruct((slots, channels), F32),
            jax.ShapeDtypeStruct((slots, state), F32),
            jax.ShapeDtypeStruct((slots, heads), F32),
        ),
        in_specs=[smem, smem] + [any_spec] * 4 + [vmem] * len(small) + [any_spec],
        out_specs=(vmem,) * 6,
        scratch_shapes=[
            VMEM((slots, span, state), BF16),
            VMEM((2, win_size, state), BF16),
            VMEM(out_weight.shape, BF16),
            VMEM((5 * slots, span), F32),
            VMEM((2, slots, span), F32),
            VMEM((2, slots, channels), F32),
            VMEM((1, span), F32),
            pltpu.SemaphoreType.DMA((slots,)),
            pltpu.SemaphoreType.DMA((2,)),
            pltpu.SemaphoreType.DMA((8,)),
        ],
        compiler_params=pltpu.CompilerParams(vmem_limit_bytes=52 * 2**20),
        name="mix",
    )(
        loops,
        live,
        *arrived,
        *small,
        out_weight,
    )

    members = lax.axis_size("tensor")
    terms = [partial] + [
        lax.ppermute(partial, "tensor", [(i, i ^ k) for i in range(members)])
        for k in range(1, members)
    ]
    states_out, windows_out = pl.pallas_call(
        state_kernel,
        out_shape=(
            jax.ShapeDtypeStruct((slots, span, state), BF16),
            jax.ShapeDtypeStruct((taps, slots, channels), BF16),
        ),
        in_specs=[smem, smem] + [any_spec] * 4 + [vmem] * 6,
        out_specs=(any_spec, vmem),
        scratch_shapes=[
            VMEM((slots, span, state), BF16),
            VMEM((slots, span, state), BF16),
            pltpu.SemaphoreType.DMA((slots,)),
            pltpu.SemaphoreType.DMA((slots,)),
        ],
        compiler_params=pltpu.CompilerParams(vmem_limit_bytes=52 * 2**20),
        cost_estimate=pl.CostEstimate(
            flops=40 * slots * span * state,
            bytes_accessed=4 * slots * span * state,
            transcendentals=0,
        ),
        name="states",
    )(loops, live, *arrived, updates, inputs, scale, last_window, order, tokens)

    terms = [term.astype(F32) for term in terms]
    while len(terms) > 1:
        terms = [terms[i] + terms[i + 1] for i in range(0, len(terms), 2)]
    mixed = terms[0].astype(BF16).reshape(2, slots, columns)
    conv_after = jnp.swapaxes(windows_out, 0, 1)[:, :, None, :]
    return mixed, states_out.reshape(ssm_state.shape), conv_after


def convolve(window_rows, conv_tokens, conv_weight, conv_bias):
    weight_rows = conv_weight.astype(jnp.float32)
    shift_rows = conv_bias.astype(jnp.float32)
    activations = []
    for step_index in range(conv_tokens.shape[0]):
        stacked = jnp.concatenate([window_rows, conv_tokens[step_index][:, None]], axis=1)
        summed = jnp.sum(stacked.astype(jnp.float32) * weight_rows[None], axis=1) + shift_rows
        activations.append(jax.nn.silu(summed))
        window_rows = stacked[:, 1:]
    return (activations, window_rows)


def advance(
    states_now,
    activations,
    dt_tokens,
    gate_tokens,
    dt_bias,
    a_log,
    skip_gain,
    norm_gain,
    heads_per_group,
):
    decay_rate = -jnp.exp(a_log)
    row_count, head_count, head_width, state_width = states_now.shape
    group_span = heads_per_group * head_width
    normed_list = []
    for step_index in range(len(activations)):
        act_rows = activations[step_index]
        group_count = act_rows.shape[1]
        values = act_rows[..., :group_span].reshape(row_count, head_count, head_width)
        input_map = jnp.repeat(
            act_rows[..., group_span : group_span + state_width], heads_per_group, axis=1
        )
        output_map = jnp.repeat(act_rows[..., group_span + state_width :], heads_per_group, axis=1)
        step_size = jax.nn.softplus(dt_tokens[step_index].astype(jnp.float32) + dt_bias)
        retained = jnp.exp(step_size * decay_rate)
        states_now = (
            retained[:, :, None, None] * states_now
            + (step_size[:, :, None] * values)[:, :, :, None] * input_map[:, :, None, :]
        )
        readout = (
            jnp.einsum("shpn,shn->shp", states_now, output_map, precision=lax.Precision.HIGHEST)
            + skip_gain[None, :, None] * values
        )
        gated_rows = readout.reshape(row_count, head_count * head_width) * jax.nn.silu(
            gate_tokens[step_index].astype(jnp.float32)
        )
        grouped = gated_rows.reshape(row_count, group_count, group_span)
        factor = lax.rsqrt(jnp.mean(grouped * grouped, axis=-1, keepdims=True) + 1e-05)
        normed = (grouped * factor).reshape(row_count, head_count * head_width) * norm_gain.astype(
            jnp.float32
        )
        normed_list.append(normed.astype(jnp.bfloat16))
    return (jnp.stack(normed_list), states_now)


def arrival_rows(received_ids, slot_count):
    wanted = jnp.arange(slot_count, dtype=jnp.int32)[:, None] == received_ids[None, :]
    buffer_index = jnp.arange(received_ids.shape[0], dtype=jnp.int32)
    return jnp.sum(jnp.where(wanted, buffer_index[None, :], 0), axis=1)


def padded(
    ssm_state,
    conv_state,
    dst_replica,
    dst_slot,
    live,
    conv_in,
    gate_in,
    dt_in,
    conv_weight,
    conv_bias,
    dt_bias,
    a_log,
    skip_gain,
    norm_gain,
    out_weight,
):
    replicas = lax.axis_size("replica")
    own_replica = lax.axis_index("replica")
    slot_count = ssm_state.shape[0]
    capacity = max(2, 2 * slot_count // replicas)
    row_index = jnp.arange(slot_count, dtype=jnp.int32)
    same_target = dst_replica[:, None] == dst_replica[None, :]
    earlier_rows = row_index[None, :] < row_index[:, None]
    member = jnp.sum(jnp.where(same_target & earlier_rows, 1, 0), axis=1).astype(jnp.int32)
    position = dst_replica * capacity + member
    buffer_rows = jnp.arange(replicas * capacity, dtype=jnp.int32)
    hit_table = position[None, :] == buffer_rows[:, None]
    picked = jnp.sum(jnp.where(hit_table, row_index[None, :], 0), axis=1)
    filled = jnp.any(hit_table, axis=1)
    send_ids = jnp.where(filled, jnp.take(dst_slot, picked), -1)
    send_windows = jnp.where(
        filled[:, None, None, None],
        jnp.take(conv_state, picked, axis=0),
        jnp.zeros((), conv_state.dtype),
    )
    send_states = jnp.where(
        filled[:, None, None, None],
        jnp.take(ssm_state, picked, axis=0),
        jnp.zeros((), ssm_state.dtype),
    )
    got_states, got_windows, got_ids = (
        lax.all_to_all(send_states, "replica", split_axis=0, concat_axis=0, tiled=True),
        lax.all_to_all(send_windows, "replica", split_axis=0, concat_axis=0, tiled=True),
        lax.all_to_all(send_ids, "replica", split_axis=0, concat_axis=0, tiled=True),
    )
    arrival = arrival_rows(got_ids, slot_count)
    windows_now = jnp.take(got_windows, arrival, axis=0)
    activations, windows_end = convolve(windows_now, conv_in, conv_weight, conv_bias)
    states_now = jnp.take(got_states, arrival, axis=0).astype(jnp.float32)
    normed_all, states_end = advance(
        states_now,
        activations,
        dt_in,
        gate_in,
        dt_bias,
        a_log,
        skip_gain,
        norm_gain,
        HEADS // GROUPS,
    )
    step_count = normed_all.shape[0]
    partial_value = jnp.dot(
        normed_all.reshape(step_count * slot_count, normed_all.shape[2]),
        out_weight,
        preferred_element_type=jnp.float32,
    )
    summed = lax.psum(partial_value, "tensor").astype(jnp.bfloat16)
    live_rows = row_index < live[own_replica]
    mixed = jnp.where(
        live_rows[None, :, None],
        summed.reshape(step_count, slot_count, summed.shape[1]),
        jnp.zeros((), jnp.bfloat16),
    )
    ssm_after = jnp.where(
        live_rows[:, None, None, None], states_end.astype(jnp.bfloat16), jnp.zeros((), jnp.bfloat16)
    )
    conv_after = jnp.where(
        live_rows[:, None, None, None], windows_end, jnp.zeros((), windows_end.dtype)
    )
    return (mixed, ssm_after, conv_after)


def solution(mesh):
    placed = (
        P(("groups", "replica"), "tensor", None, None),
        P(("groups", "replica"), None, "tensor", None),
        P(("groups", "replica")),
        P(("groups", "replica")),
        P("groups"),
        P(None, ("groups", "replica"), "tensor", None),
        P(None, ("groups", "replica"), "tensor"),
        P(None, ("groups", "replica"), "tensor"),
        P(None, "tensor", None),
        P("tensor", None),
        P("tensor"),
        P("tensor"),
        P("tensor"),
        P("tensor"),
        P("tensor", None),
    )
    shards = routed if mesh.shape["replica"] == 4 else padded
    return jax.shard_map(
        shards,
        mesh=mesh,
        in_specs=placed,
        out_specs=(
            P(None, ("groups", "replica"), None),
            P(("groups", "replica"), "tensor", None, None),
            P(("groups", "replica"), None, "tensor", None),
        ),
        check_vma=False,
    )
```

```python
import functools
import itertools

import jax
import jax.numpy as jnp
from jax import lax
from jax.experimental import pallas as pl
from jax.experimental.pallas import tpu as pltpu
from jax.sharding import PartitionSpec as P

HEADS = 64
GROUPS = 4
BF16 = jnp.bfloat16
F32 = jnp.float32
SMEM = pltpu.SMEM
VMEM = pltpu.VMEM


def send_graphs(replicas):
    pairs = list(itertools.combinations(range(replicas), 2))
    graphs = []
    for chosen in itertools.product(pairs, repeat=replicas):
        if any(sum(d in pair for pair in chosen) != 2 for d in range(replicas)):
            continue
        for picks in itertools.product((0, 1), repeat=replicas):
            first = [chosen[s][picks[s]] for s in range(replicas)]
            if len(set(first)) == replicas:
                second = [chosen[s][1 - picks[s]] for s in range(replicas)]
                break
        code = sum(1 << (replicas * s + d) for s in range(replicas) for d in chosen[s])
        bits = sum(picks[s] << s for s in range(replicas))
        graphs.append((code, bits, first, second))
    return graphs


def parts_of(value, count):
    out = []
    for _ in range(count):
        part = value.astype(BF16).astype(F32)
        out.append(part)
        value = value - part
    return out


def sum_of_parts(rows, count):
    size = rows.shape[0] // count
    total = rows[:size]
    for part in range(1, count):
        total = total + rows[part * size : (part + 1) * size]
    return total


def silu(value):
    return value / (1.0 + jnp.exp(-value))


def softplus(value):
    return jnp.maximum(value, 0.0) + jnp.log1p(jnp.exp(-jnp.abs(value)))


def prepare(small, wide, scale, gate, begun, gains):
    dt, tokens, gates, weights, bias, dt_shift, rates, skips, norms = small
    slots, heads = scale.shape
    span = wide.shape[1]
    steps, kept = [], []
    for step in range(2):
        steps.append(softplus(dt[step] + dt_shift))
        kept.append(jnp.exp(steps[step] * -jnp.exp(rates)))
    scale[...] = kept[0] * kept[1]
    per_head = jnp.concatenate(steps + kept + [jnp.broadcast_to(skips, (slots, heads))], axis=0)
    head_of = lax.div(lax.broadcasted_iota(jnp.int32, (heads, span), 1), span // heads)
    spread = jnp.where(
        head_of == lax.broadcasted_iota(jnp.int32, (heads, span), 0), 1.0, 0.0
    ).astype(BF16)
    wide[...] = sum_of_parts(
        jnp.dot(
            jnp.concatenate(parts_of(per_head, 3), axis=0).astype(BF16),
            spread,
            preferred_element_type=F32,
        ),
        3,
    )
    taps = weights.shape[0] - 1
    begun[0] = tokens[0] * weights[taps : taps + 1] + bias
    begun[1] = tokens[0] * weights[taps - 1 : taps] + tokens[1] * weights[taps : taps + 1] + bias
    for step in range(2):
        gate[step] = silu(gates[step])
    gains[...] = jnp.concatenate([norms[k : k + 1] for k in range(norms.shape[0])], axis=1)


def near_kernel(states_in, windows_in, states, windows, sems):
    copies = [
        pltpu.make_async_copy(states_in.at[row], states.at[row], sems.at[row])
        for row in range(states.shape[0])
    ]
    for copy in copies:
        copy.start()
    windows[...] = windows_in[...].astype(F32)
    for copy in copies:
        copy.wait()


def route_kernel(graphs, replicas, slots, *refs):
    to_replica, to_slot, *others = refs[: replicas + 1]
    states, windows, buf_a, buf_b, branch, loops, win_rows, sems = refs[replicas + 1 :]
    half = slots // 2
    span = states.shape[1]
    taps = windows.shape[0]
    lanes = states.shape[2]
    block = win_rows.shape[1]
    me = lax.axis_index("replica")
    sources = [lax.rem(me + (replicas - k), replicas) for k in range(replicas)]
    edges = jnp.int32(0)
    for i in range(slots):
        edges = edges + jnp.left_shift(jnp.int32(1), to_replica[i])
    code = jnp.left_shift(lax.div(edges, jnp.int32(half)), me * replicas)
    for k, other in enumerate(others, 1):
        flags = jnp.left_shift(jnp.int32(1), other[...]).astype(F32)
        edges = jnp.sum(flags).astype(jnp.int32)
        code = code + jnp.left_shift(lax.div(edges, jnp.int32(half)), sources[k] * replicas)
    index = jnp.int32(0)
    bits = jnp.int32(0)
    for j, (graph_code, graph_bits, _, _) in enumerate(graphs):
        hit = code == graph_code
        index = jnp.where(hit, j, index)
        bits = jnp.where(hit, graph_bits, bits)
    branch[0] = index

    def second_matching(source, target):
        row = lax.bitwise_and(
            lax.shift_right_logical(code, source * replicas), jnp.int32((1 << replicas) - 1)
        )
        below = lax.bitwise_and(row, jnp.left_shift(jnp.int32(1), target) - 1)
        rank = jnp.where(below != 0, 1, 0)
        pick = lax.bitwise_and(lax.shift_right_logical(bits, source), jnp.int32(1))
        return jnp.where(rank == pick, 0, 1)

    def pack(buf, place, i):
        rows = pl.ds(pl.multiple_of(place * span, span), span)
        return pltpu.make_async_copy(states.at[i], buf.at[rows], sems.at[i])

    counts = [jnp.int32(0), jnp.int32(0)]
    picked = []
    for i in range(slots):
        which = second_matching(me, to_replica[i])
        place = jnp.where(which == 0, counts[0], counts[1])
        counts = [counts[0] + (1 - which), counts[1] + which]
        picked.append((which, place))
        for m, buf in enumerate((buf_a, buf_b)):

            @pl.when(which == m)
            def _(buf=buf, i=i, place=place):
                pack(buf, place, i).start()

    loop = lax.bitwise_and(lax.shift_right_logical(code, me * replicas + me), jnp.int32(1))
    second = second_matching(me, me)
    loops[0] = loop * (1 - second)
    loops[1] = loop * second

    win_rows[...] = jnp.zeros_like(win_rows)
    for tap in range(taps):
        for i in range(slots):
            which, place = picked[i]
            win_rows[which, pl.ds(tap * half + place, 1), :] = windows[tap, i : i + 1, :]
    for i in range(slots):
        which, place = picked[i]
        win_rows[which, pl.ds(taps * half + place, 1), :] = jnp.full(
            (1, win_rows.shape[2]), to_slot[i].astype(F32)
        )
    for m, buf in enumerate((buf_a, buf_b)):
        rows = win_rows[m].astype(BF16)
        for part in range(rows.shape[1] // lanes):
            top = half * span + part * block
            buf[top : top + block, :] = rows[:, part * lanes : (part + 1) * lanes]

    for i in range(slots):
        pack(buf_a, 0, i).wait()


def fetch_rows(loops, pairs, held, sems):
    _, span, _ = held.shape
    half = held.shape[0] // 2
    for m, sources in enumerate(pairs):
        for own, source in enumerate(sources):

            @pl.when(loops[m] == own)
            def _(m=m, source=source):
                for member in range(half):
                    row = m * half + member
                    pltpu.make_async_copy(
                        source.at[pl.ds(member * span, span)], held.at[row], sems.at[row]
                    ).start()


def row_wait(pairs, held, sems, row):
    rows = pl.ds(0, held.shape[1])
    pltpu.make_async_copy(pairs[0][0].at[rows], held.at[row], sems.at[row]).wait()


def mix_kernel(
    loops,
    live,
    got_a,
    got_b,
    own_a,
    own_b,
    dt_in,
    conv_in,
    gate_in,
    conv_weight,
    conv_bias,
    dt_bias,
    a_log,
    skip_gain,
    norm_gain,
    out_weight,
    partial,
    updates,
    inputs,
    last_window,
    order,
    scale,
    held,
    win_held,
    weight_held,
    wide,
    gate,
    begun,
    gains,
    in_sem,
    win_sem,
    weight_sem,
):
    slots, span, state = held.shape
    half = slots // 2
    taps = conv_weight.shape[0] - 1
    pairs = ((got_a, own_a), (got_b, own_b))
    win_size = win_held.shape[1]
    block = win_size // (begun.shape[2] // state)

    for m, sources in enumerate(pairs):
        for own, source in enumerate(sources):

            @pl.when(loops[m] == own)
            def _(m=m, source=source):
                pltpu.make_async_copy(
                    source.at[pl.ds(half * span, win_size)], win_held.at[m], win_sem.at[m]
                ).start()

    fetch_rows(loops, pairs, held, in_sem)
    chunk = out_weight.shape[0] // weight_sem.shape[0]
    fetches = []
    for part in range(weight_sem.shape[0]):
        rows = pl.ds(part * chunk, chunk)
        fetches.append(
            pltpu.make_async_copy(out_weight.at[rows], weight_held.at[rows], weight_sem.at[part])
        )
        fetches[part].start(priority=1)

    small = (
        dt_in, conv_in, gate_in, conv_weight, conv_bias, dt_bias, a_log, skip_gain, norm_gain,
    )
    prepare([ref[...].astype(F32) for ref in small], wide, scale, gate, begun, gains)

    for m in range(len(pairs)):
        pltpu.make_async_copy(
            got_a.at[pl.ds(half * span, win_size)], win_held.at[m], win_sem.at[m]
        ).wait()
    parts = []
    for part in range(win_size // block):
        cut = slice(part * block, (part + 1) * block)
        parts.append(jnp.concatenate([win_held[m, cut, :] for m in range(len(pairs))], axis=0))
    top = taps * half
    arrived = [parts[0][m * block + top : m * block + top + half].astype(F32) for m in range(len(pairs))]
    order[...] = jnp.concatenate(arrived, axis=0)
    shape = (len(pairs) * block, taps * slots)
    column = lax.broadcasted_iota(jnp.int32, shape, 1)
    tap_of = lax.div(lax.rem(lax.broadcasted_iota(jnp.int32, shape, 0), block), half)
    slot_at = jnp.concatenate(
        [rows[:, : taps * slots] for rows in arrived for _ in range(block // half)], axis=0
    )
    choose = jnp.where(
        (tap_of == lax.div(column, slots)) & (slot_at == lax.rem(column, slots).astype(F32)),
        1.0,
        0.0,
    ).astype(BF16)
    windows = lax.dot_general(
        choose,
        jnp.concatenate(parts, axis=1),
        (((0,), (0,)), ((), ())),
        preferred_element_type=F32,
    )
    line = [windows[tap * slots : (tap + 1) * slots] for tap in range(taps)]
    last_window[...] = line[taps - 1]

    weights = conv_weight[...].astype(F32)
    acts = []
    for step in range(2):
        total = begun[step]
        for tap in range(taps - step):
            total = total + line[step + tap] * weights[tap : tap + 1]
        acts.append(silu(total))
    xs = [act[:, :span] for act in acts]
    bs = [act[:, span : span + state] for act in acts]
    cs = [act[:, span + state :] for act in acts]
    step_size = [wide[:slots], wide[slots : 2 * slots]]
    retained = [wide[2 * slots : 3 * slots], wide[3 * slots : 4 * slots]]
    skip = wide[4 * slots :]
    us = [step_size[0] * xs[0], step_size[1] * xs[1]]
    updates[0] = retained[1] * us[0]
    updates[1] = us[1]
    inputs[0] = bs[0]
    inputs[1] = bs[1]
    queries = jnp.concatenate(parts_of(jnp.concatenate(cs, axis=0), 3), axis=0).astype(BF16)
    row_of = lax.rem(lax.broadcasted_iota(jnp.int32, (2 * slots, span), 0), slots).astype(F32)
    slot_of = jnp.concatenate(arrived, axis=0)[:, :1]

    ys = jnp.zeros((2 * slots, span), F32)
    for row in range(slots):
        if row % (slots // 2) == 0:
            for later in range(row, row + (slots // 2)):
                row_wait(pairs, held, in_sem, later)
        got = lax.dot_general(
            queries, held[row], (((1,), (1,)), ((), ())), preferred_element_type=F32
        )
        ys = jnp.where(row_of == slot_of[row : row + 1], sum_of_parts(got, 3), ys)

    def dots(b, c):
        return jnp.sum(b * c, axis=1, keepdims=True)

    reads = [
        retained[0] * ys[:slots] + us[0] * dots(bs[0], cs[0]) + skip * xs[0],
        retained[1] * (retained[0] * ys[slots:] + us[0] * dots(bs[0], cs[1]))
        + us[1] * dots(bs[1], cs[1])
        + skip * xs[1],
    ]
    normed = []
    for step in range(2):
        gated = reads[step] * gate[step]
        factor = lax.rsqrt(jnp.sum(gated * gated, axis=1, keepdims=True) * (1.0 / span) + 1e-05)
        normed.append((gated * factor) * gains[...])
    normed = jnp.concatenate(normed, axis=0)
    alive = live[lax.axis_index("replica")].astype(F32)
    normed = jnp.where(row_of < alive, normed, 0.0).astype(BF16)
    total = None
    for part, fetch in enumerate(fetches):
        fetch.wait()
        cut = slice(part * chunk, (part + 1) * chunk)
        term = jnp.dot(normed[:, cut], weight_held[cut, :], preferred_element_type=F32)
        total = term if total is None else total + term
    partial[...] = total.astype(BF16)


def state_kernel(
    loops,
    live,
    got_a,
    got_b,
    own_a,
    own_b,
    updates,
    inputs,
    scale,
    last_window,
    order,
    conv_in,
    states_out,
    windows_out,
    held,
    held_out,
    in_sem,
    out_sem,
):
    slots, span, state = held.shape
    heads = scale.shape[1]
    width = span // heads
    pairs = ((got_a, own_a), (got_b, own_b))
    fetch_rows(loops, pairs, held, in_sem)
    slot_of = [jnp.max(order[row : row + 1, :]).astype(jnp.int32) for row in range(slots)]
    alive = live[lax.axis_index("replica")]
    keep = lax.broadcasted_iota(jnp.int32, last_window.shape, 0) < alive
    for tap, tokens in enumerate(
        (last_window[...], conv_in[0].astype(F32), conv_in[1].astype(F32))
    ):
        windows_out[tap] = jnp.where(keep, tokens, 0.0).astype(BF16)

    u_parts, b_parts = [], []
    for step in range(2):
        u_hi, u_lo = parts_of(updates[step], 2)
        b_hi, b_lo = parts_of(inputs[step], 2)
        u_parts += [u_hi, u_hi, u_lo, u_lo]
        b_parts += [b_hi, b_lo, b_hi, b_lo]
    u_columns = jnp.transpose(jnp.concatenate(u_parts, axis=0)).astype(BF16)
    b_rows = jnp.concatenate(b_parts, axis=0)
    b_of = lax.rem(lax.broadcasted_iota(jnp.int32, b_rows.shape, 0), slots)
    for row in range(slots):
        slot = slot_of[row]
        factors = scale[pl.ds(slot, 1), :]
        if row % (slots // 2) == 0:
            for later in range(row, row + (slots // 2)):
                row_wait(pairs, held, in_sem, later)
        added = jnp.dot(
            u_columns,
            jnp.where(b_of == slot, b_rows, 0.0).astype(BF16),
            preferred_element_type=F32,
        )
        for head in range(heads):
            rows = slice(head * width, (head + 1) * width)
            value = (
                factors[:, head : head + 1] * held[row, rows, :].astype(F32)
                + added[rows]
            )
            held_out[row, rows, :] = jnp.where(slot < alive, value, 0.0).astype(BF16)
        pltpu.make_async_copy(held_out.at[row], states_out.at[slot], out_sem.at[row]).start()
    for row in range(slots):
        pltpu.make_async_copy(held_out.at[row], states_out.at[row], out_sem.at[row]).wait()


def routed(
    ssm_state,
    conv_state,
    dst_replica,
    dst_slot,
    live,
    conv_in,
    gate_in,
    dt_in,
    conv_weight,
    conv_bias,
    dt_bias,
    a_log,
    skip_gain,
    norm_gain,
    out_weight,
):
    replicas = lax.axis_size("replica")
    slots, heads, width, state = ssm_state.shape
    half = slots // 2
    span = heads * width
    taps, channels = conv_state.shape[1], conv_state.shape[3]
    columns = out_weight.shape[1]
    graphs = send_graphs(replicas)
    block = 16 * pl.cdiv(half * (taps + 1), 16)
    win_size = block * (channels // state)

    mine = dst_replica.reshape(1, slots)
    others = [
        lax.ppermute(mine, "replica", [(s, (s + k) % replicas) for s in range(replicas)])
        for k in range(1, replicas)
    ]
    tokens = conv_in.reshape(2, slots, channels)

    any_spec = pl.BlockSpec(memory_space=pl.ANY)
    smem = pl.BlockSpec(memory_space=SMEM)
    vmem = pl.BlockSpec(memory_space=VMEM)
    packed = jax.ShapeDtypeStruct((half * span + win_size, state), BF16)
    weights = conv_weight.reshape(taps + 1, channels)
    lanes = 128
    small = (
        dt_in,
        tokens,
        gate_in,
        weights,
        conv_bias,
        dt_bias.reshape(1, heads),
        a_log.reshape(1, heads),
        skip_gain.reshape(1, heads),
        norm_gain.reshape(span // lanes, lanes),
    )
    f32 = lambda *shape: jax.ShapeDtypeStruct(shape, F32)
    states, windows = pl.pallas_call(
        near_kernel,
        out_shape=(
            jax.ShapeDtypeStruct((slots, span, state), BF16),
            f32(taps, slots, channels),
        ),
        in_specs=[any_spec, vmem],
        out_specs=(vmem, vmem),
        scratch_shapes=[pltpu.SemaphoreType.DMA((slots,))],
        compiler_params=pltpu.CompilerParams(vmem_limit_bytes=16 * 2**20),
        name="near",
    )(
        ssm_state.reshape(slots, span, state),
        jnp.swapaxes(conv_state, 0, 1).reshape(taps, slots, channels),
    )

    own_a, own_b, branch, loops = pl.pallas_call(
        functools.partial(route_kernel, graphs, replicas, slots),
        out_shape=(
            packed,
            packed,
            jax.ShapeDtypeStruct((1,), jnp.int32),
            jax.ShapeDtypeStruct((2,), jnp.int32),
        ),
        in_specs=[smem] * 2 + [vmem] * (replicas + 1),
        out_specs=(vmem, vmem, smem, smem),
        scratch_shapes=[VMEM((2, block, channels), F32), pltpu.SemaphoreType.DMA((slots,))],
        compiler_params=pltpu.CompilerParams(vmem_limit_bytes=16 * 2**20),
        name="route",
    )(dst_replica, dst_slot, *others, states, windows)

    def along(first, second):
        def send(rows_a, rows_b):
            out = []
            for value, targets in ((rows_a, first), (rows_b, second)):
                moves = [(s, d) for s, d in enumerate(targets) if s != d]
                out.append(lax.ppermute(value, "replica", moves) if moves else value)
            return tuple(out)

        return send

    branches = tuple(
        jax.make_jaxpr(along(first, second))(own_a, own_b) for _, _, first, second in graphs
    )
    got_a, got_b = lax.cond_p.bind(branch[0], own_a, own_b, branches=branches)
    arrived = (got_a, got_b, own_a, own_b)

    partial, updates, inputs, last_window, order, scale = pl.pallas_call(
        mix_kernel,
        out_shape=(
            jax.ShapeDtypeStruct((2 * slots, columns), BF16),
            jax.ShapeDtypeStruct((2, slots, span), F32),
            jax.ShapeDtypeStruct((2, slots, state), F32),
            jax.ShapeDtypeStruct((slots, channels), F32),
            jax.ShapeDtypeStruct((slots, state), F32),
            jax.ShapeDtypeStruct((slots, heads), F32),
        ),
        in_specs=[smem, smem] + [any_spec] * 4 + [vmem] * len(small) + [any_spec],
        out_specs=(vmem,) * 6,
        scratch_shapes=[
            VMEM((slots, span, state), BF16),
            VMEM((2, win_size, state), BF16),
            VMEM(out_weight.shape, BF16),
            VMEM((5 * slots, span), F32),
            VMEM((2, slots, span), F32),
            VMEM((2, slots, channels), F32),
            VMEM((1, span), F32),
            pltpu.SemaphoreType.DMA((slots,)),
            pltpu.SemaphoreType.DMA((2,)),
            pltpu.SemaphoreType.DMA((8,)),
        ],
        compiler_params=pltpu.CompilerParams(vmem_limit_bytes=52 * 2**20),
        name="mix",
    )(
        loops,
        live,
        *arrived,
        *small,
        out_weight,
    )

    members = lax.axis_size("tensor")
    terms = [partial] + [
        lax.ppermute(partial, "tensor", [(i, i ^ k) for i in range(members)])
        for k in range(1, members)
    ]
    states_out, windows_out = pl.pallas_call(
        state_kernel,
        out_shape=(
            jax.ShapeDtypeStruct((slots, span, state), BF16),
            jax.ShapeDtypeStruct((taps, slots, channels), BF16),
        ),
        in_specs=[smem, smem] + [any_spec] * 4 + [vmem] * 6,
        out_specs=(any_spec, vmem),
        scratch_shapes=[
            VMEM((slots, span, state), BF16),
            VMEM((slots, span, state), BF16),
            pltpu.SemaphoreType.DMA((slots,)),
            pltpu.SemaphoreType.DMA((slots,)),
        ],
        compiler_params=pltpu.CompilerParams(vmem_limit_bytes=52 * 2**20),
        cost_estimate=pl.CostEstimate(
            flops=40 * slots * span * state,
            bytes_accessed=4 * slots * span * state,
            transcendentals=0,
        ),
        name="states",
    )(loops, live, *arrived, updates, inputs, scale, last_window, order, tokens)

    terms = [term.astype(F32) for term in terms]
    while len(terms) > 1:
        terms = [terms[i] + terms[i + 1] for i in range(0, len(terms), 2)]
    mixed = terms[0].astype(BF16).reshape(2, slots, columns)
    conv_after = jnp.swapaxes(windows_out, 0, 1)[:, :, None, :]
    return mixed, states_out.reshape(ssm_state.shape), conv_after


def convolve(window_rows, conv_tokens, conv_weight, conv_bias):
    weight_rows = conv_weight.astype(jnp.float32)
    shift_rows = conv_bias.astype(jnp.float32)
    activations = []
    for step_index in range(conv_tokens.shape[0]):
        stacked = jnp.concatenate([window_rows, conv_tokens[step_index][:, None]], axis=1)
        summed = jnp.sum(stacked.astype(jnp.float32) * weight_rows[None], axis=1) + shift_rows
        activations.append(jax.nn.silu(summed))
        window_rows = stacked[:, 1:]
    return (activations, window_rows)


def advance(
    states_now,
    activations,
    dt_tokens,
    gate_tokens,
    dt_bias,
    a_log,
    skip_gain,
    norm_gain,
    heads_per_group,
):
    decay_rate = -jnp.exp(a_log)
    row_count, head_count, head_width, state_width = states_now.shape
    group_span = heads_per_group * head_width
    normed_list = []
    for step_index in range(len(activations)):
        act_rows = activations[step_index]
        group_count = act_rows.shape[1]
        values = act_rows[..., :group_span].reshape(row_count, head_count, head_width)
        input_map = jnp.repeat(
            act_rows[..., group_span : group_span + state_width], heads_per_group, axis=1
        )
        output_map = jnp.repeat(act_rows[..., group_span + state_width :], heads_per_group, axis=1)
        step_size = jax.nn.softplus(dt_tokens[step_index].astype(jnp.float32) + dt_bias)
        retained = jnp.exp(step_size * decay_rate)
        states_now = (
            retained[:, :, None, None] * states_now
            + (step_size[:, :, None] * values)[:, :, :, None] * input_map[:, :, None, :]
        )
        readout = (
            jnp.einsum("shpn,shn->shp", states_now, output_map, precision=lax.Precision.HIGHEST)
            + skip_gain[None, :, None] * values
        )
        gated_rows = readout.reshape(row_count, head_count * head_width) * jax.nn.silu(
            gate_tokens[step_index].astype(jnp.float32)
        )
        grouped = gated_rows.reshape(row_count, group_count, group_span)
        factor = lax.rsqrt(jnp.mean(grouped * grouped, axis=-1, keepdims=True) + 1e-05)
        normed = (grouped * factor).reshape(row_count, head_count * head_width) * norm_gain.astype(
            jnp.float32
        )
        normed_list.append(normed.astype(jnp.bfloat16))
    return (jnp.stack(normed_list), states_now)


def arrival_rows(received_ids, slot_count):
    wanted = jnp.arange(slot_count, dtype=jnp.int32)[:, None] == received_ids[None, :]
    buffer_index = jnp.arange(received_ids.shape[0], dtype=jnp.int32)
    return jnp.sum(jnp.where(wanted, buffer_index[None, :], 0), axis=1)


def padded(
    ssm_state,
    conv_state,
    dst_replica,
    dst_slot,
    live,
    conv_in,
    gate_in,
    dt_in,
    conv_weight,
    conv_bias,
    dt_bias,
    a_log,
    skip_gain,
    norm_gain,
    out_weight,
):
    replicas = lax.axis_size("replica")
    own_replica = lax.axis_index("replica")
    slot_count = ssm_state.shape[0]
    capacity = max(2, 2 * slot_count // replicas)
    row_index = jnp.arange(slot_count, dtype=jnp.int32)
    same_target = dst_replica[:, None] == dst_replica[None, :]
    earlier_rows = row_index[None, :] < row_index[:, None]
    member = jnp.sum(jnp.where(same_target & earlier_rows, 1, 0), axis=1).astype(jnp.int32)
    position = dst_replica * capacity + member
    buffer_rows = jnp.arange(replicas * capacity, dtype=jnp.int32)
    hit_table = position[None, :] == buffer_rows[:, None]
    picked = jnp.sum(jnp.where(hit_table, row_index[None, :], 0), axis=1)
    filled = jnp.any(hit_table, axis=1)
    send_ids = jnp.where(filled, jnp.take(dst_slot, picked), -1)
    send_windows = jnp.where(
        filled[:, None, None, None],
        jnp.take(conv_state, picked, axis=0),
        jnp.zeros((), conv_state.dtype),
    )
    send_states = jnp.where(
        filled[:, None, None, None],
        jnp.take(ssm_state, picked, axis=0),
        jnp.zeros((), ssm_state.dtype),
    )
    got_states, got_windows, got_ids = (
        lax.all_to_all(send_states, "replica", split_axis=0, concat_axis=0, tiled=True),
        lax.all_to_all(send_windows, "replica", split_axis=0, concat_axis=0, tiled=True),
        lax.all_to_all(send_ids, "replica", split_axis=0, concat_axis=0, tiled=True),
    )
    arrival = arrival_rows(got_ids, slot_count)
    windows_now = jnp.take(got_windows, arrival, axis=0)
    activations, windows_end = convolve(windows_now, conv_in, conv_weight, conv_bias)
    states_now = jnp.take(got_states, arrival, axis=0).astype(jnp.float32)
    normed_all, states_end = advance(
        states_now,
        activations,
        dt_in,
        gate_in,
        dt_bias,
        a_log,
        skip_gain,
        norm_gain,
        HEADS // GROUPS,
    )
    step_count = normed_all.shape[0]
    partial_value = jnp.dot(
        normed_all.reshape(step_count * slot_count, normed_all.shape[2]),
        out_weight,
        preferred_element_type=jnp.float32,
    )
    summed = lax.psum(partial_value, "tensor").astype(jnp.bfloat16)
    live_rows = row_index < live[own_replica]
    mixed = jnp.where(
        live_rows[None, :, None],
        summed.reshape(step_count, slot_count, summed.shape[1]),
        jnp.zeros((), jnp.bfloat16),
    )
    ssm_after = jnp.where(
        live_rows[:, None, None, None], states_end.astype(jnp.bfloat16), jnp.zeros((), jnp.bfloat16)
    )
    conv_after = jnp.where(
        live_rows[:, None, None, None], windows_end, jnp.zeros((), windows_end.dtype)
    )
    return (mixed, ssm_after, conv_after)


def solution(mesh):
    placed = (
        P(("groups", "replica"), "tensor", None, None),
        P(("groups", "replica"), None, "tensor", None),
        P(("groups", "replica")),
        P(("groups", "replica")),
        P("groups"),
        P(None, ("groups", "replica"), "tensor", None),
        P(None, ("groups", "replica"), "tensor"),
        P(None, ("groups", "replica"), "tensor"),
        P(None, "tensor", None),
        P("tensor", None),
        P("tensor"),
        P("tensor"),
        P("tensor"),
        P("tensor"),
        P("tensor", None),
    )
    shards = routed if mesh.shape["replica"] == 4 else padded
    return jax.shard_map(
        shards,
        mesh=mesh,
        in_specs=placed,
        out_specs=(
            P(None, ("groups", "replica"), None),
            P(("groups", "replica"), "tensor", None, None),
            P(("groups", "replica"), None, "tensor", None),
        ),
        check_vma=False,
    )
```

```python
import functools
import itertools

import jax
import jax.numpy as jnp
from jax import lax
from jax.experimental import pallas as pl
from jax.experimental.pallas import tpu as pltpu
from jax.sharding import PartitionSpec as P

HEADS = 64
GROUPS = 4
BF16 = jnp.bfloat16
F32 = jnp.float32
SMEM = pltpu.SMEM
VMEM = pltpu.VMEM


def send_graphs(replicas):
    pairs = list(itertools.combinations(range(replicas), 2))
    graphs = []
    for chosen in itertools.product(pairs, repeat=replicas):
        if any(sum(d in pair for pair in chosen) != 2 for d in range(replicas)):
            continue
        for picks in itertools.product((0, 1), repeat=replicas):
            first = [chosen[s][picks[s]] for s in range(replicas)]
            if len(set(first)) == replicas:
                second = [chosen[s][1 - picks[s]] for s in range(replicas)]
                break
        code = sum(1 << (replicas * s + d) for s in range(replicas) for d in chosen[s])
        bits = sum(picks[s] << s for s in range(replicas))
        graphs.append((code, bits, first, second))
    return graphs


def parts_of(value, count):
    out = []
    for _ in range(count):
        part = value.astype(BF16).astype(F32)
        out.append(part)
        value = value - part
    return out


def sum_of_parts(rows, count):
    size = rows.shape[0] // count
    total = rows[:size]
    for part in range(1, count):
        total = total + rows[part * size : (part + 1) * size]
    return total


def silu(value):
    return value / (1.0 + jnp.exp(-value))


def softplus(value):
    return jnp.maximum(value, 0.0) + jnp.log1p(jnp.exp(-jnp.abs(value)))


def prepare(small, wide, scale, gate, begun, gains):
    dt, tokens, gates, weights, bias, dt_shift, rates, skips, norms = small
    slots, heads = scale.shape
    span = wide.shape[1]
    steps, kept = [], []
    for step in range(2):
        steps.append(softplus(dt[step] + dt_shift))
        kept.append(jnp.exp(steps[step] * -jnp.exp(rates)))
    scale[...] = kept[0] * kept[1]
    per_head = jnp.concatenate(steps + kept + [jnp.broadcast_to(skips, (slots, heads))], axis=0)
    head_of = lax.div(lax.broadcasted_iota(jnp.int32, (heads, span), 1), span // heads)
    spread = jnp.where(
        head_of == lax.broadcasted_iota(jnp.int32, (heads, span), 0), 1.0, 0.0
    ).astype(BF16)
    wide[...] = sum_of_parts(
        jnp.dot(
            jnp.concatenate(parts_of(per_head, 3), axis=0).astype(BF16),
            spread,
            preferred_element_type=F32,
        ),
        3,
    )
    taps = weights.shape[0] - 1
    begun[0] = tokens[0] * weights[taps : taps + 1] + bias
    begun[1] = tokens[0] * weights[taps - 1 : taps] + tokens[1] * weights[taps : taps + 1] + bias
    for step in range(2):
        gate[step] = silu(gates[step])
    gains[...] = jnp.concatenate([norms[k : k + 1] for k in range(norms.shape[0])], axis=1)


def near_kernel(states_in, windows_in, states, windows, sems):
    copies = [
        pltpu.make_async_copy(states_in.at[row], states.at[row], sems.at[row])
        for row in range(states.shape[0])
    ]
    for copy in copies:
        copy.start()
    windows[...] = windows_in[...].astype(F32)
    for copy in copies:
        copy.wait()


def route_kernel(graphs, replicas, slots, *refs):
    to_replica, to_slot, *others = refs[: replicas + 1]
    states, windows, buf_a, buf_b, branch, loops, win_rows, packed, sems = refs[replicas + 1 :]
    half = slots // 2
    span = states.shape[1]
    taps = windows.shape[0]
    lanes = states.shape[2]
    me = lax.axis_index("replica")
    sources = [lax.rem(me + (replicas - k), replicas) for k in range(replicas)]
    edges = jnp.int32(0)
    for i in range(slots):
        edges = edges + jnp.left_shift(jnp.int32(1), to_replica[i])
    code = jnp.left_shift(lax.div(edges, jnp.int32(half)), me * replicas)
    for k, other in enumerate(others, 1):
        flags = jnp.left_shift(jnp.int32(1), other[...]).astype(F32)
        edges = jnp.sum(flags).astype(jnp.int32)
        code = code + jnp.left_shift(lax.div(edges, jnp.int32(half)), sources[k] * replicas)
    index = jnp.int32(0)
    bits = jnp.int32(0)
    for j, (graph_code, graph_bits, _, _) in enumerate(graphs):
        hit = code == graph_code
        index = jnp.where(hit, j, index)
        bits = jnp.where(hit, graph_bits, bits)
    branch[0] = index

    def second_matching(source, target):
        row = lax.bitwise_and(
            lax.shift_right_logical(code, source * replicas), jnp.int32((1 << replicas) - 1)
        )
        below = lax.bitwise_and(row, jnp.left_shift(jnp.int32(1), target) - 1)
        rank = jnp.where(below != 0, 1, 0)
        pick = lax.bitwise_and(lax.shift_right_logical(bits, source), jnp.int32(1))
        return jnp.where(rank == pick, 0, 1)

    def pack(buf, place, i):
        rows = pl.ds(pl.multiple_of(place * span, span), span)
        return pltpu.make_async_copy(states.at[i], buf.at[rows], sems.at[i])

    counts = [jnp.int32(0), jnp.int32(0)]
    picked = []
    for i in range(slots):
        which = second_matching(me, to_replica[i])
        place = jnp.where(which == 0, counts[0], counts[1])
        counts = [counts[0] + (1 - which), counts[1] + which]
        picked.append((which, place))
        for m, buf in enumerate((buf_a, buf_b)):

            @pl.when(which == m)
            def _(buf=buf, i=i, place=place):
                pack(buf, place, i).start()

    loop = lax.bitwise_and(lax.shift_right_logical(code, me * replicas + me), jnp.int32(1))
    second = second_matching(me, me)
    loops[0] = loop * (1 - second)
    loops[1] = loop * second

    packed[...] = jnp.zeros_like(packed)
    for tap in range(taps):
        for i in range(slots):
            which, place = picked[i]
            win_rows[which, pl.ds(tap * half + place, 1), :] = windows[tap, i : i + 1, :]
    for i in range(slots):
        which, place = picked[i]
        win_rows[which, pl.ds(taps * half + place, 1), :] = jnp.full(
            (1, win_rows.shape[2]), to_slot[i].astype(F32)
        )
    lines = taps * half
    parts = win_rows.shape[2] // lanes
    for m, buf in enumerate((buf_a, buf_b)):
        for part in range(parts):
            packed[m, part * lines : (part + 1) * lines, :] = win_rows[
                m, :lines, part * lanes : (part + 1) * lanes
            ]
        packed[m, parts * lines : parts * lines + half, :] = win_rows[
            m, lines : lines + half, :lanes
        ]
        buf[half * span :, :] = packed[m].astype(BF16)

    for i in range(slots):
        pack(buf_a, 0, i).wait()


def fetch_rows(loops, pairs, held, sems):
    _, span, _ = held.shape
    half = held.shape[0] // 2
    for m, sources in enumerate(pairs):
        for own, source in enumerate(sources):

            @pl.when(loops[m] == own)
            def _(m=m, source=source):
                for member in range(half):
                    row = m * half + member
                    pltpu.make_async_copy(
                        source.at[pl.ds(member * span, span)], held.at[row], sems.at[row]
                    ).start()


def row_wait(pairs, held, sems, row):
    rows = pl.ds(0, held.shape[1])
    pltpu.make_async_copy(pairs[0][0].at[rows], held.at[row], sems.at[row]).wait()


def mix_kernel(
    loops,
    live,
    got_a,
    got_b,
    own_a,
    own_b,
    dt_in,
    conv_in,
    gate_in,
    conv_weight,
    conv_bias,
    dt_bias,
    a_log,
    skip_gain,
    norm_gain,
    out_weight,
    partial,
    updates,
    inputs,
    last_window,
    order,
    scale,
    held,
    win_held,
    weight_held,
    wide,
    gate,
    begun,
    gains,
    in_sem,
    win_sem,
    weight_sem,
):
    slots, span, state = held.shape
    half = slots // 2
    taps = conv_weight.shape[0] - 1
    pairs = ((got_a, own_a), (got_b, own_b))
    win_size = win_held.shape[1]

    for m, sources in enumerate(pairs):
        for own, source in enumerate(sources):

            @pl.when(loops[m] == own)
            def _(m=m, source=source):
                pltpu.make_async_copy(
                    source.at[pl.ds(half * span, win_size)], win_held.at[m], win_sem.at[m]
                ).start()

    fetch_rows(loops, pairs, held, in_sem)
    chunk = out_weight.shape[0] // weight_sem.shape[0]
    fetches = []
    for part in range(weight_sem.shape[0]):
        rows = pl.ds(part * chunk, chunk)
        fetches.append(
            pltpu.make_async_copy(out_weight.at[rows], weight_held.at[rows], weight_sem.at[part])
        )
        fetches[part].start(priority=1)

    small = (
        dt_in, conv_in, gate_in, conv_weight, conv_bias, dt_bias, a_log, skip_gain, norm_gain,
    )
    prepare([ref[...].astype(F32) for ref in small], wide, scale, gate, begun, gains)

    for m in range(len(pairs)):
        pltpu.make_async_copy(
            got_a.at[pl.ds(half * span, win_size)], win_held.at[m], win_sem.at[m]
        ).wait()
    lines = taps * half
    count = begun.shape[2] // state
    brought = [win_held[m].astype(F32) for m in range(len(pairs))]
    parts = [
        jnp.concatenate([rows[part * lines : (part + 1) * lines] for rows in brought], axis=0)
        for part in range(count)
    ]
    arrived = [rows[count * lines : count * lines + half] for rows in brought]
    order[...] = jnp.concatenate(arrived, axis=0)
    shape = (len(pairs) * lines, taps * slots)
    column = lax.broadcasted_iota(jnp.int32, shape, 1)
    tap_of = lax.div(lax.rem(lax.broadcasted_iota(jnp.int32, shape, 0), lines), half)
    slot_at = jnp.concatenate(
        [rows[:, : taps * slots] for rows in arrived for _ in range(taps)], axis=0
    )
    choose = jnp.where(
        (tap_of == lax.div(column, slots)) & (slot_at == lax.rem(column, slots).astype(F32)),
        1.0,
        0.0,
    ).astype(BF16)
    windows = lax.dot_general(
        choose,
        jnp.concatenate(parts, axis=1).astype(BF16),
        (((0,), (0,)), ((), ())),
        preferred_element_type=F32,
    )
    line = [windows[tap * slots : (tap + 1) * slots] for tap in range(taps)]
    last_window[...] = line[taps - 1]

    weights = conv_weight[...].astype(F32)
    acts = []
    for step in range(2):
        total = begun[step]
        for tap in range(taps - step):
            total = total + line[step + tap] * weights[tap : tap + 1]
        acts.append(silu(total))
    xs = [act[:, :span] for act in acts]
    bs = [act[:, span : span + state] for act in acts]
    cs = [act[:, span + state :] for act in acts]
    step_size = [wide[:slots], wide[slots : 2 * slots]]
    retained = [wide[2 * slots : 3 * slots], wide[3 * slots : 4 * slots]]
    skip = wide[4 * slots :]
    us = [step_size[0] * xs[0], step_size[1] * xs[1]]
    updates[0] = retained[1] * us[0]
    updates[1] = us[1]
    inputs[0] = bs[0]
    inputs[1] = bs[1]
    queries = jnp.concatenate(parts_of(jnp.concatenate(cs, axis=0), 3), axis=0).astype(BF16)
    row_of = lax.rem(lax.broadcasted_iota(jnp.int32, (2 * slots, span), 0), slots).astype(F32)
    slot_of = jnp.concatenate(arrived, axis=0)[:, :1]

    ys = jnp.zeros((2 * slots, span), F32)
    for row in range(slots):
        if row % (slots // 2) == 0:
            for later in range(row, row + (slots // 2)):
                row_wait(pairs, held, in_sem, later)
        got = lax.dot_general(
            queries, held[row], (((1,), (1,)), ((), ())), preferred_element_type=F32
        )
        ys = jnp.where(row_of == slot_of[row : row + 1], sum_of_parts(got, 3), ys)

    def dots(b, c):
        return jnp.sum(b * c, axis=1, keepdims=True)

    reads = [
        retained[0] * ys[:slots] + us[0] * dots(bs[0], cs[0]) + skip * xs[0],
        retained[1] * (retained[0] * ys[slots:] + us[0] * dots(bs[0], cs[1]))
        + us[1] * dots(bs[1], cs[1])
        + skip * xs[1],
    ]
    normed = []
    for step in range(2):
        gated = reads[step] * gate[step]
        factor = lax.rsqrt(jnp.sum(gated * gated, axis=1, keepdims=True) * (1.0 / span) + 1e-05)
        normed.append((gated * factor) * gains[...])
    normed = jnp.concatenate(normed, axis=0)
    alive = live[lax.axis_index("replica")].astype(F32)
    normed = jnp.where(row_of < alive, normed, 0.0).astype(BF16)
    total = None
    for part, fetch in enumerate(fetches):
        fetch.wait()
        cut = slice(part * chunk, (part + 1) * chunk)
        term = jnp.dot(normed[:, cut], weight_held[cut, :], preferred_element_type=F32)
        total = term if total is None else total + term
    partial[...] = total.astype(BF16)


def state_kernel(
    loops,
    live,
    got_a,
    got_b,
    own_a,
    own_b,
    updates,
    inputs,
    scale,
    last_window,
    order,
    conv_in,
    states_out,
    windows_out,
    held,
    held_out,
    in_sem,
    out_sem,
):
    slots, span, state = held.shape
    heads = scale.shape[1]
    width = span // heads
    pairs = ((got_a, own_a), (got_b, own_b))
    fetch_rows(loops, pairs, held, in_sem)
    slot_of = [jnp.max(order[row : row + 1, :]).astype(jnp.int32) for row in range(slots)]
    alive = live[lax.axis_index("replica")]
    keep = lax.broadcasted_iota(jnp.int32, last_window.shape, 0) < alive
    for tap, tokens in enumerate(
        (last_window[...], conv_in[0].astype(F32), conv_in[1].astype(F32))
    ):
        windows_out[tap] = jnp.where(keep, tokens, 0.0).astype(BF16)

    u_parts, b_parts = [], []
    for step in range(2):
        u_hi, u_lo = parts_of(updates[step], 2)
        b_hi, b_lo = parts_of(inputs[step], 2)
        u_parts += [u_hi, u_hi, u_lo, u_lo]
        b_parts += [b_hi, b_lo, b_hi, b_lo]
    u_columns = jnp.transpose(jnp.concatenate(u_parts, axis=0)).astype(BF16)
    b_rows = jnp.concatenate(b_parts, axis=0)
    b_of = lax.rem(lax.broadcasted_iota(jnp.int32, b_rows.shape, 0), slots)
    for row in range(slots):
        slot = slot_of[row]
        factors = scale[pl.ds(slot, 1), :]
        if row % (slots // 2) == 0:
            for later in range(row, row + (slots // 2)):
                row_wait(pairs, held, in_sem, later)
        added = jnp.dot(
            u_columns,
            jnp.where(b_of == slot, b_rows, 0.0).astype(BF16),
            preferred_element_type=F32,
        )
        for head in range(heads):
            rows = slice(head * width, (head + 1) * width)
            value = (
                factors[:, head : head + 1] * held[row, rows, :].astype(F32)
                + added[rows]
            )
            held_out[row, rows, :] = jnp.where(slot < alive, value, 0.0).astype(BF16)
        pltpu.make_async_copy(held_out.at[row], states_out.at[slot], out_sem.at[row]).start()
    for row in range(slots):
        pltpu.make_async_copy(held_out.at[row], states_out.at[row], out_sem.at[row]).wait()


def routed(
    ssm_state,
    conv_state,
    dst_replica,
    dst_slot,
    live,
    conv_in,
    gate_in,
    dt_in,
    conv_weight,
    conv_bias,
    dt_bias,
    a_log,
    skip_gain,
    norm_gain,
    out_weight,
):
    replicas = lax.axis_size("replica")
    slots, heads, width, state = ssm_state.shape
    half = slots // 2
    span = heads * width
    taps, channels = conv_state.shape[1], conv_state.shape[3]
    columns = out_weight.shape[1]
    graphs = send_graphs(replicas)
    block = 16 * pl.cdiv(half * (taps + 1), 16)
    win_size = 16 * pl.cdiv(half * taps * (channels // state) + half, 16)

    mine = dst_replica.reshape(1, slots)
    others = [
        lax.ppermute(mine, "replica", [(s, (s + k) % replicas) for s in range(replicas)])
        for k in range(1, replicas)
    ]
    tokens = conv_in.reshape(2, slots, channels)

    any_spec = pl.BlockSpec(memory_space=pl.ANY)
    smem = pl.BlockSpec(memory_space=SMEM)
    vmem = pl.BlockSpec(memory_space=VMEM)
    packed = jax.ShapeDtypeStruct((half * span + win_size, state), BF16)
    weights = conv_weight.reshape(taps + 1, channels)
    lanes = 128
    small = (
        dt_in,
        tokens,
        gate_in,
        weights,
        conv_bias,
        dt_bias.reshape(1, heads),
        a_log.reshape(1, heads),
        skip_gain.reshape(1, heads),
        norm_gain.reshape(span // lanes, lanes),
    )
    f32 = lambda *shape: jax.ShapeDtypeStruct(shape, F32)
    states, windows = pl.pallas_call(
        near_kernel,
        out_shape=(
            jax.ShapeDtypeStruct((slots, span, state), BF16),
            f32(taps, slots, channels),
        ),
        in_specs=[any_spec, vmem],
        out_specs=(vmem, vmem),
        scratch_shapes=[pltpu.SemaphoreType.DMA((slots,))],
        compiler_params=pltpu.CompilerParams(vmem_limit_bytes=16 * 2**20),
        name="near",
    )(
        ssm_state.reshape(slots, span, state),
        jnp.swapaxes(conv_state, 0, 1).reshape(taps, slots, channels),
    )

    own_a, own_b, branch, loops = pl.pallas_call(
        functools.partial(route_kernel, graphs, replicas, slots),
        out_shape=(
            packed,
            packed,
            jax.ShapeDtypeStruct((1,), jnp.int32),
            jax.ShapeDtypeStruct((2,), jnp.int32),
        ),
        in_specs=[smem] * 2 + [vmem] * (replicas + 1),
        out_specs=(vmem, vmem, smem, smem),
        scratch_shapes=[
            VMEM((2, block, channels), F32),
            VMEM((2, win_size, state), F32),
            pltpu.SemaphoreType.DMA((slots,)),
        ],
        compiler_params=pltpu.CompilerParams(vmem_limit_bytes=16 * 2**20),
        name="route",
    )(dst_replica, dst_slot, *others, states, windows)

    def along(first, second):
        def send(rows_a, rows_b):
            out = []
            for value, targets in ((rows_a, first), (rows_b, second)):
                moves = [(s, d) for s, d in enumerate(targets) if s != d]
                out.append(lax.ppermute(value, "replica", moves) if moves else value)
            return tuple(out)

        return send

    branches = tuple(
        jax.make_jaxpr(along(first, second))(own_a, own_b) for _, _, first, second in graphs
    )
    got_a, got_b = lax.cond_p.bind(branch[0], own_a, own_b, branches=branches)
    arrived = (got_a, got_b, own_a, own_b)

    partial, updates, inputs, last_window, order, scale = pl.pallas_call(
        mix_kernel,
        out_shape=(
            jax.ShapeDtypeStruct((2 * slots, columns), BF16),
            jax.ShapeDtypeStruct((2, slots, span), F32),
            jax.ShapeDtypeStruct((2, slots, state), F32),
            jax.ShapeDtypeStruct((slots, channels), F32),
            jax.ShapeDtypeStruct((slots, state), F32),
            jax.ShapeDtypeStruct((slots, heads), F32),
        ),
        in_specs=[smem, smem] + [any_spec] * 4 + [vmem] * len(small) + [any_spec],
        out_specs=(vmem,) * 6,
        scratch_shapes=[
            VMEM((slots, span, state), BF16),
            VMEM((2, win_size, state), BF16),
            VMEM(out_weight.shape, BF16),
            VMEM((5 * slots, span), F32),
            VMEM((2, slots, span), F32),
            VMEM((2, slots, channels), F32),
            VMEM((1, span), F32),
            pltpu.SemaphoreType.DMA((slots,)),
            pltpu.SemaphoreType.DMA((2,)),
            pltpu.SemaphoreType.DMA((8,)),
        ],
        compiler_params=pltpu.CompilerParams(vmem_limit_bytes=52 * 2**20),
        name="mix",
    )(
        loops,
        live,
        *arrived,
        *small,
        out_weight,
    )

    members = lax.axis_size("tensor")
    terms = [partial] + [
        lax.ppermute(partial, "tensor", [(i, i ^ k) for i in range(members)])
        for k in range(1, members)
    ]
    states_out, windows_out = pl.pallas_call(
        state_kernel,
        out_shape=(
            jax.ShapeDtypeStruct((slots, span, state), BF16),
            jax.ShapeDtypeStruct((taps, slots, channels), BF16),
        ),
        in_specs=[smem, smem] + [any_spec] * 4 + [vmem] * 6,
        out_specs=(any_spec, vmem),
        scratch_shapes=[
            VMEM((slots, span, state), BF16),
            VMEM((slots, span, state), BF16),
            pltpu.SemaphoreType.DMA((slots,)),
            pltpu.SemaphoreType.DMA((slots,)),
        ],
        compiler_params=pltpu.CompilerParams(vmem_limit_bytes=52 * 2**20),
        cost_estimate=pl.CostEstimate(
            flops=40 * slots * span * state,
            bytes_accessed=4 * slots * span * state,
            transcendentals=0,
        ),
        name="states",
    )(loops, live, *arrived, updates, inputs, scale, last_window, order, tokens)

    terms = [term.astype(F32) for term in terms]
    while len(terms) > 1:
        terms = [terms[i] + terms[i + 1] for i in range(0, len(terms), 2)]
    mixed = terms[0].astype(BF16).reshape(2, slots, columns)
    conv_after = jnp.swapaxes(windows_out, 0, 1)[:, :, None, :]
    return mixed, states_out.reshape(ssm_state.shape), conv_after


def convolve(window_rows, conv_tokens, conv_weight, conv_bias):
    weight_rows = conv_weight.astype(jnp.float32)
    shift_rows = conv_bias.astype(jnp.float32)
    activations = []
    for step_index in range(conv_tokens.shape[0]):
        stacked = jnp.concatenate([window_rows, conv_tokens[step_index][:, None]], axis=1)
        summed = jnp.sum(stacked.astype(jnp.float32) * weight_rows[None], axis=1) + shift_rows
        activations.append(jax.nn.silu(summed))
        window_rows = stacked[:, 1:]
    return (activations, window_rows)


def advance(
    states_now,
    activations,
    dt_tokens,
    gate_tokens,
    dt_bias,
    a_log,
    skip_gain,
    norm_gain,
    heads_per_group,
):
    decay_rate = -jnp.exp(a_log)
    row_count, head_count, head_width, state_width = states_now.shape
    group_span = heads_per_group * head_width
    normed_list = []
    for step_index in range(len(activations)):
        act_rows = activations[step_index]
        group_count = act_rows.shape[1]
        values = act_rows[..., :group_span].reshape(row_count, head_count, head_width)
        input_map = jnp.repeat(
            act_rows[..., group_span : group_span + state_width], heads_per_group, axis=1
        )
        output_map = jnp.repeat(act_rows[..., group_span + state_width :], heads_per_group, axis=1)
        step_size = jax.nn.softplus(dt_tokens[step_index].astype(jnp.float32) + dt_bias)
        retained = jnp.exp(step_size * decay_rate)
        states_now = (
            retained[:, :, None, None] * states_now
            + (step_size[:, :, None] * values)[:, :, :, None] * input_map[:, :, None, :]
        )
        readout = (
            jnp.einsum("shpn,shn->shp", states_now, output_map, precision=lax.Precision.HIGHEST)
            + skip_gain[None, :, None] * values
        )
        gated_rows = readout.reshape(row_count, head_count * head_width) * jax.nn.silu(
            gate_tokens[step_index].astype(jnp.float32)
        )
        grouped = gated_rows.reshape(row_count, group_count, group_span)
        factor = lax.rsqrt(jnp.mean(grouped * grouped, axis=-1, keepdims=True) + 1e-05)
        normed = (grouped * factor).reshape(row_count, head_count * head_width) * norm_gain.astype(
            jnp.float32
        )
        normed_list.append(normed.astype(jnp.bfloat16))
    return (jnp.stack(normed_list), states_now)


def arrival_rows(received_ids, slot_count):
    wanted = jnp.arange(slot_count, dtype=jnp.int32)[:, None] == received_ids[None, :]
    buffer_index = jnp.arange(received_ids.shape[0], dtype=jnp.int32)
    return jnp.sum(jnp.where(wanted, buffer_index[None, :], 0), axis=1)


def padded(
    ssm_state,
    conv_state,
    dst_replica,
    dst_slot,
    live,
    conv_in,
    gate_in,
    dt_in,
    conv_weight,
    conv_bias,
    dt_bias,
    a_log,
    skip_gain,
    norm_gain,
    out_weight,
):
    replicas = lax.axis_size("replica")
    own_replica = lax.axis_index("replica")
    slot_count = ssm_state.shape[0]
    capacity = max(2, 2 * slot_count // replicas)
    row_index = jnp.arange(slot_count, dtype=jnp.int32)
    same_target = dst_replica[:, None] == dst_replica[None, :]
    earlier_rows = row_index[None, :] < row_index[:, None]
    member = jnp.sum(jnp.where(same_target & earlier_rows, 1, 0), axis=1).astype(jnp.int32)
    position = dst_replica * capacity + member
    buffer_rows = jnp.arange(replicas * capacity, dtype=jnp.int32)
    hit_table = position[None, :] == buffer_rows[:, None]
    picked = jnp.sum(jnp.where(hit_table, row_index[None, :], 0), axis=1)
    filled = jnp.any(hit_table, axis=1)
    send_ids = jnp.where(filled, jnp.take(dst_slot, picked), -1)
    send_windows = jnp.where(
        filled[:, None, None, None],
        jnp.take(conv_state, picked, axis=0),
        jnp.zeros((), conv_state.dtype),
    )
    send_states = jnp.where(
        filled[:, None, None, None],
        jnp.take(ssm_state, picked, axis=0),
        jnp.zeros((), ssm_state.dtype),
    )
    got_states, got_windows, got_ids = (
        lax.all_to_all(send_states, "replica", split_axis=0, concat_axis=0, tiled=True),
        lax.all_to_all(send_windows, "replica", split_axis=0, concat_axis=0, tiled=True),
        lax.all_to_all(send_ids, "replica", split_axis=0, concat_axis=0, tiled=True),
    )
    arrival = arrival_rows(got_ids, slot_count)
    windows_now = jnp.take(got_windows, arrival, axis=0)
    activations, windows_end = convolve(windows_now, conv_in, conv_weight, conv_bias)
    states_now = jnp.take(got_states, arrival, axis=0).astype(jnp.float32)
    normed_all, states_end = advance(
        states_now,
        activations,
        dt_in,
        gate_in,
        dt_bias,
        a_log,
        skip_gain,
        norm_gain,
        HEADS // GROUPS,
    )
    step_count = normed_all.shape[0]
    partial_value = jnp.dot(
        normed_all.reshape(step_count * slot_count, normed_all.shape[2]),
        out_weight,
        preferred_element_type=jnp.float32,
    )
    summed = lax.psum(partial_value, "tensor").astype(jnp.bfloat16)
    live_rows = row_index < live[own_replica]
    mixed = jnp.where(
        live_rows[None, :, None],
        summed.reshape(step_count, slot_count, summed.shape[1]),
        jnp.zeros((), jnp.bfloat16),
    )
    ssm_after = jnp.where(
        live_rows[:, None, None, None], states_end.astype(jnp.bfloat16), jnp.zeros((), jnp.bfloat16)
    )
    conv_after = jnp.where(
        live_rows[:, None, None, None], windows_end, jnp.zeros((), windows_end.dtype)
    )
    return (mixed, ssm_after, conv_after)


def solution(mesh):
    placed = (
        P(("groups", "replica"), "tensor", None, None),
        P(("groups", "replica"), None, "tensor", None),
        P(("groups", "replica")),
        P(("groups", "replica")),
        P("groups"),
        P(None, ("groups", "replica"), "tensor", None),
        P(None, ("groups", "replica"), "tensor"),
        P(None, ("groups", "replica"), "tensor"),
        P(None, "tensor", None),
        P("tensor", None),
        P("tensor"),
        P("tensor"),
        P("tensor"),
        P("tensor"),
        P("tensor", None),
    )
    shards = routed if mesh.shape["replica"] == 4 else padded
    return jax.shard_map(
        shards,
        mesh=mesh,
        in_specs=placed,
        out_specs=(
            P(None, ("groups", "replica"), None),
            P(("groups", "replica"), "tensor", None, None),
            P(("groups", "replica"), None, "tensor", None),
        ),
        check_vma=False,
    )
```

```python
import functools
import itertools

import jax
import jax.numpy as jnp
from jax import lax
from jax.experimental import pallas as pl
from jax.experimental.pallas import tpu as pltpu
from jax.sharding import PartitionSpec as P

HEADS = 64
GROUPS = 4
BF16 = jnp.bfloat16
F32 = jnp.float32
SMEM = pltpu.SMEM
VMEM = pltpu.VMEM


def send_graphs(replicas):
    pairs = list(itertools.combinations(range(replicas), 2))
    graphs = []
    for chosen in itertools.product(pairs, repeat=replicas):
        if any(sum(d in pair for pair in chosen) != 2 for d in range(replicas)):
            continue
        for picks in itertools.product((0, 1), repeat=replicas):
            first = [chosen[s][picks[s]] for s in range(replicas)]
            if len(set(first)) == replicas:
                second = [chosen[s][1 - picks[s]] for s in range(replicas)]
                break
        code = sum(1 << (replicas * s + d) for s in range(replicas) for d in chosen[s])
        bits = sum(picks[s] << s for s in range(replicas))
        graphs.append((code, bits, first, second))
    return graphs


def parts_of(value, count):
    out = []
    for _ in range(count):
        part = value.astype(BF16).astype(F32)
        out.append(part)
        value = value - part
    return out


def sum_of_parts(rows, count):
    size = rows.shape[0] // count
    total = rows[:size]
    for part in range(1, count):
        total = total + rows[part * size : (part + 1) * size]
    return total


def silu(value):
    return value / (1.0 + jnp.exp(-value))


def softplus(value):
    return jnp.maximum(value, 0.0) + jnp.log1p(jnp.exp(-jnp.abs(value)))


def prepare(small, wide, scale, gate, begun, gains):
    dt, tokens, gates, weights, bias, dt_shift, rates, skips, norms = small
    slots, heads = scale.shape
    span = wide.shape[1]
    steps, kept = [], []
    for step in range(2):
        steps.append(softplus(dt[step] + dt_shift))
        kept.append(jnp.exp(steps[step] * -jnp.exp(rates)))
    scale[...] = kept[0] * kept[1]
    per_head = jnp.concatenate(steps + kept + [jnp.broadcast_to(skips, (slots, heads))], axis=0)
    head_of = lax.div(lax.broadcasted_iota(jnp.int32, (heads, span), 1), span // heads)
    spread = jnp.where(
        head_of == lax.broadcasted_iota(jnp.int32, (heads, span), 0), 1.0, 0.0
    ).astype(BF16)
    wide[...] = sum_of_parts(
        jnp.dot(
            jnp.concatenate(parts_of(per_head, 3), axis=0).astype(BF16),
            spread,
            preferred_element_type=F32,
        ),
        3,
    )
    taps = weights.shape[0] - 1
    begun[0] = tokens[0] * weights[taps : taps + 1] + bias
    begun[1] = tokens[0] * weights[taps - 1 : taps] + tokens[1] * weights[taps : taps + 1] + bias
    for step in range(2):
        gate[step] = silu(gates[step])
    gains[...] = jnp.concatenate([norms[k : k + 1] for k in range(norms.shape[0])], axis=1)


def near_kernel(states_in, windows_in, states, windows, sems):
    copies = [
        pltpu.make_async_copy(states_in.at[row], states.at[row], sems.at[row])
        for row in range(states.shape[0])
    ]
    for copy in copies:
        copy.start()
    windows[...] = windows_in[...].astype(F32)
    for copy in copies:
        copy.wait()


def route_kernel(graphs, replicas, slots, *refs):
    to_replica, to_slot, *others = refs[: replicas + 1]
    states, windows, buf_a, buf_b, branch, loops, win_rows, packed, sems = refs[replicas + 1 :]
    half = slots // 2
    span = states.shape[1]
    taps = windows.shape[0]
    lanes = states.shape[2]
    me = lax.axis_index("replica")
    sources = [lax.rem(me + (replicas - k), replicas) for k in range(replicas)]
    edges = jnp.int32(0)
    for i in range(slots):
        edges = edges + jnp.left_shift(jnp.int32(1), to_replica[i])
    code = jnp.left_shift(lax.div(edges, jnp.int32(half)), me * replicas)
    for k, other in enumerate(others, 1):
        flags = jnp.left_shift(jnp.int32(1), other[...]).astype(F32)
        edges = jnp.sum(flags).astype(jnp.int32)
        code = code + jnp.left_shift(lax.div(edges, jnp.int32(half)), sources[k] * replicas)
    found = jnp.int32(0)
    for j, (graph_code, graph_bits, _, _) in enumerate(graphs):
        hit = code == graph_code
        found = jnp.where(hit, j + (graph_bits << 8), found)
    index = lax.bitwise_and(found, jnp.int32(255))
    bits = lax.shift_right_logical(found, 8)
    branch[0] = index

    def second_matching(source, target):
        row = lax.bitwise_and(
            lax.shift_right_logical(code, source * replicas), jnp.int32((1 << replicas) - 1)
        )
        below = lax.bitwise_and(row, jnp.left_shift(jnp.int32(1), target) - 1)
        rank = jnp.where(below != 0, 1, 0)
        pick = lax.bitwise_and(lax.shift_right_logical(bits, source), jnp.int32(1))
        return jnp.where(rank == pick, 0, 1)

    def pack(buf, place, i):
        rows = pl.ds(pl.multiple_of(place * span, span), span)
        return pltpu.make_async_copy(states.at[i], buf.at[rows], sems.at[i])

    counts = [jnp.int32(0), jnp.int32(0)]
    picked = []
    for i in range(slots):
        which = second_matching(me, to_replica[i])
        place = jnp.where(which == 0, counts[0], counts[1])
        counts = [counts[0] + (1 - which), counts[1] + which]
        picked.append((which, place))
        for m, buf in enumerate((buf_a, buf_b)):

            @pl.when(which == m)
            def _(buf=buf, i=i, place=place):
                pack(buf, place, i).start()

    loop = lax.bitwise_and(lax.shift_right_logical(code, me * replicas + me), jnp.int32(1))
    second = second_matching(me, me)
    loops[0] = loop * (1 - second)
    loops[1] = loop * second

    packed[...] = jnp.zeros_like(packed)
    for tap in range(taps):
        for i in range(slots):
            which, place = picked[i]
            win_rows[which, pl.ds(tap * half + place, 1), :] = windows[tap, i : i + 1, :]
    for i in range(slots):
        which, place = picked[i]
        win_rows[which, pl.ds(taps * half + place, 1), :] = jnp.full(
            (1, win_rows.shape[2]), to_slot[i].astype(F32)
        )
    lines = taps * half
    parts = win_rows.shape[2] // lanes
    for m, buf in enumerate((buf_a, buf_b)):
        for part in range(parts):
            packed[m, part * lines : (part + 1) * lines, :] = win_rows[
                m, :lines, part * lanes : (part + 1) * lanes
            ]
        packed[m, parts * lines : parts * lines + half, :] = win_rows[
            m, lines : lines + half, :lanes
        ]
        buf[half * span :, :] = packed[m].astype(BF16)

    for i in range(slots):
        pack(buf_a, 0, i).wait()


def fetch_rows(loops, pairs, held, sems):
    _, span, _ = held.shape
    half = held.shape[0] // 2
    for m, sources in enumerate(pairs):
        for own, source in enumerate(sources):

            @pl.when(loops[m] == own)
            def _(m=m, source=source):
                for member in range(half):
                    row = m * half + member
                    pltpu.make_async_copy(
                        source.at[pl.ds(member * span, span)], held.at[row], sems.at[row]
                    ).start()


def row_wait(pairs, held, sems, row):
    rows = pl.ds(0, held.shape[1])
    pltpu.make_async_copy(pairs[0][0].at[rows], held.at[row], sems.at[row]).wait()


def mix_kernel(
    loops,
    live,
    got_a,
    got_b,
    own_a,
    own_b,
    dt_in,
    conv_in,
    gate_in,
    conv_weight,
    conv_bias,
    dt_bias,
    a_log,
    skip_gain,
    norm_gain,
    out_weight,
    partial,
    updates,
    inputs,
    last_window,
    order,
    scale,
    held,
    win_held,
    weight_held,
    wide,
    gate,
    begun,
    gains,
    in_sem,
    win_sem,
    weight_sem,
):
    slots, span, state = held.shape
    half = slots // 2
    taps = conv_weight.shape[0] - 1
    pairs = ((got_a, own_a), (got_b, own_b))
    win_size = win_held.shape[1]

    for m, sources in enumerate(pairs):
        for own, source in enumerate(sources):

            @pl.when(loops[m] == own)
            def _(m=m, source=source):
                pltpu.make_async_copy(
                    source.at[pl.ds(half * span, win_size)], win_held.at[m], win_sem.at[m]
                ).start()

    fetch_rows(loops, pairs, held, in_sem)
    chunk = out_weight.shape[0] // weight_sem.shape[0]
    fetches = []
    for part in range(weight_sem.shape[0]):
        rows = pl.ds(part * chunk, chunk)
        fetches.append(
            pltpu.make_async_copy(out_weight.at[rows], weight_held.at[rows], weight_sem.at[part])
        )
        fetches[part].start(priority=1)

    small = (
        dt_in, conv_in, gate_in, conv_weight, conv_bias, dt_bias, a_log, skip_gain, norm_gain,
    )
    prepare([ref[...].astype(F32) for ref in small], wide, scale, gate, begun, gains)

    for m in range(len(pairs)):
        pltpu.make_async_copy(
            got_a.at[pl.ds(half * span, win_size)], win_held.at[m], win_sem.at[m]
        ).wait()
    lines = taps * half
    count = begun.shape[2] // state
    brought = [win_held[m].astype(F32) for m in range(len(pairs))]
    parts = [
        jnp.concatenate([rows[part * lines : (part + 1) * lines] for rows in brought], axis=0)
        for part in range(count)
    ]
    arrived = [rows[count * lines : count * lines + half] for rows in brought]
    order[...] = jnp.concatenate(arrived, axis=0)
    shape = (len(pairs) * lines, taps * slots)
    column = lax.broadcasted_iota(jnp.int32, shape, 1)
    tap_of = lax.div(lax.rem(lax.broadcasted_iota(jnp.int32, shape, 0), lines), half)
    slot_at = jnp.concatenate(
        [rows[:, : taps * slots] for rows in arrived for _ in range(taps)], axis=0
    )
    choose = jnp.where(
        (tap_of == lax.div(column, slots)) & (slot_at == lax.rem(column, slots).astype(F32)),
        1.0,
        0.0,
    ).astype(BF16)
    windows = lax.dot_general(
        choose,
        jnp.concatenate(parts, axis=1).astype(BF16),
        (((0,), (0,)), ((), ())),
        preferred_element_type=F32,
    )
    line = [windows[tap * slots : (tap + 1) * slots] for tap in range(taps)]
    last_window[...] = line[taps - 1]

    weights = conv_weight[...].astype(F32)
    acts = []
    for step in range(2):
        total = begun[step]
        for tap in range(taps - step):
            total = total + line[step + tap] * weights[tap : tap + 1]
        acts.append(silu(total))
    xs = [act[:, :span] for act in acts]
    bs = [act[:, span : span + state] for act in acts]
    cs = [act[:, span + state :] for act in acts]
    step_size = [wide[:slots], wide[slots : 2 * slots]]
    retained = [wide[2 * slots : 3 * slots], wide[3 * slots : 4 * slots]]
    skip = wide[4 * slots :]
    us = [step_size[0] * xs[0], step_size[1] * xs[1]]
    updates[0] = retained[1] * us[0]
    updates[1] = us[1]
    inputs[0] = bs[0]
    inputs[1] = bs[1]
    queries = jnp.concatenate(parts_of(jnp.concatenate(cs, axis=0), 3), axis=0).astype(BF16)
    row_of = lax.rem(lax.broadcasted_iota(jnp.int32, (2 * slots, span), 0), slots).astype(F32)
    slot_of = jnp.concatenate(arrived, axis=0)[:, :1]

    ys = jnp.zeros((2 * slots, span), F32)
    for row in range(slots):
        if row % (slots // 2) == 0:
            for later in range(row, row + (slots // 2)):
                row_wait(pairs, held, in_sem, later)
        got = lax.dot_general(
            queries, held[row], (((1,), (1,)), ((), ())), preferred_element_type=F32
        )
        ys = jnp.where(row_of == slot_of[row : row + 1], sum_of_parts(got, 3), ys)

    def dots(b, c):
        return jnp.sum(b * c, axis=1, keepdims=True)

    reads = [
        retained[0] * ys[:slots] + us[0] * dots(bs[0], cs[0]) + skip * xs[0],
        retained[1] * (retained[0] * ys[slots:] + us[0] * dots(bs[0], cs[1]))
        + us[1] * dots(bs[1], cs[1])
        + skip * xs[1],
    ]
    normed = []
    for step in range(2):
        gated = reads[step] * gate[step]
        factor = lax.rsqrt(jnp.sum(gated * gated, axis=1, keepdims=True) * (1.0 / span) + 1e-05)
        normed.append((gated * factor) * gains[...])
    normed = jnp.concatenate(normed, axis=0)
    alive = live[lax.axis_index("replica")].astype(F32)
    normed = jnp.where(row_of < alive, normed, 0.0).astype(BF16)
    total = None
    for part, fetch in enumerate(fetches):
        fetch.wait()
        cut = slice(part * chunk, (part + 1) * chunk)
        term = jnp.dot(normed[:, cut], weight_held[cut, :], preferred_element_type=F32)
        total = term if total is None else total + term
    partial[...] = total.astype(BF16)


def state_kernel(
    loops,
    live,
    got_a,
    got_b,
    own_a,
    own_b,
    updates,
    inputs,
    scale,
    last_window,
    order,
    conv_in,
    states_out,
    windows_out,
    held,
    held_out,
    in_sem,
    out_sem,
):
    slots, span, state = held.shape
    heads = scale.shape[1]
    width = span // heads
    pairs = ((got_a, own_a), (got_b, own_b))
    fetch_rows(loops, pairs, held, in_sem)
    slot_of = [jnp.max(order[row : row + 1, :]).astype(jnp.int32) for row in range(slots)]
    alive = live[lax.axis_index("replica")]
    keep = lax.broadcasted_iota(jnp.int32, last_window.shape, 0) < alive
    for tap, tokens in enumerate(
        (last_window[...], conv_in[0].astype(F32), conv_in[1].astype(F32))
    ):
        windows_out[tap] = jnp.where(keep, tokens, 0.0).astype(BF16)

    u_parts, b_parts = [], []
    for step in range(2):
        u_hi, u_lo = parts_of(updates[step], 2)
        b_hi, b_lo = parts_of(inputs[step], 2)
        u_parts += [u_hi, u_hi, u_lo, u_lo]
        b_parts += [b_hi, b_lo, b_hi, b_lo]
    u_columns = jnp.transpose(jnp.concatenate(u_parts, axis=0)).astype(BF16)
    b_rows = jnp.concatenate(b_parts, axis=0)
    b_of = lax.rem(lax.broadcasted_iota(jnp.int32, b_rows.shape, 0), slots)
    for row in range(slots):
        slot = slot_of[row]
        factors = scale[pl.ds(slot, 1), :]
        if row % (slots // 2) == 0:
            for later in range(row, row + (slots // 2)):
                row_wait(pairs, held, in_sem, later)
        added = jnp.dot(
            u_columns,
            jnp.where(b_of == slot, b_rows, 0.0).astype(BF16),
            preferred_element_type=F32,
        )
        for head in range(heads):
            rows = slice(head * width, (head + 1) * width)
            value = (
                factors[:, head : head + 1] * held[row, rows, :].astype(F32)
                + added[rows]
            )
            held_out[row, rows, :] = jnp.where(slot < alive, value, 0.0).astype(BF16)
        pltpu.make_async_copy(held_out.at[row], states_out.at[slot], out_sem.at[row]).start()
    for row in range(slots):
        pltpu.make_async_copy(held_out.at[row], states_out.at[row], out_sem.at[row]).wait()


def routed(
    ssm_state,
    conv_state,
    dst_replica,
    dst_slot,
    live,
    conv_in,
    gate_in,
    dt_in,
    conv_weight,
    conv_bias,
    dt_bias,
    a_log,
    skip_gain,
    norm_gain,
    out_weight,
):
    replicas = lax.axis_size("replica")
    slots, heads, width, state = ssm_state.shape
    half = slots // 2
    span = heads * width
    taps, channels = conv_state.shape[1], conv_state.shape[3]
    columns = out_weight.shape[1]
    graphs = send_graphs(replicas)
    block = 16 * pl.cdiv(half * (taps + 1), 16)
    win_size = 16 * pl.cdiv(half * taps * (channels // state) + half, 16)

    mine = dst_replica.reshape(1, slots)
    others = [
        lax.ppermute(mine, "replica", [(s, (s + k) % replicas) for s in range(replicas)])
        for k in range(1, replicas)
    ]
    tokens = conv_in.reshape(2, slots, channels)

    any_spec = pl.BlockSpec(memory_space=pl.ANY)
    smem = pl.BlockSpec(memory_space=SMEM)
    vmem = pl.BlockSpec(memory_space=VMEM)
    packed = jax.ShapeDtypeStruct((half * span + win_size, state), BF16)
    weights = conv_weight.reshape(taps + 1, channels)
    lanes = 128
    small = (
        dt_in,
        tokens,
        gate_in,
        weights,
        conv_bias,
        dt_bias.reshape(1, heads),
        a_log.reshape(1, heads),
        skip_gain.reshape(1, heads),
        norm_gain.reshape(span // lanes, lanes),
    )
    f32 = lambda *shape: jax.ShapeDtypeStruct(shape, F32)
    states, windows = pl.pallas_call(
        near_kernel,
        out_shape=(
            jax.ShapeDtypeStruct((slots, span, state), BF16),
            f32(taps, slots, channels),
        ),
        in_specs=[any_spec, vmem],
        out_specs=(vmem, vmem),
        scratch_shapes=[pltpu.SemaphoreType.DMA((slots,))],
        compiler_params=pltpu.CompilerParams(vmem_limit_bytes=16 * 2**20),
        name="near",
    )(
        ssm_state.reshape(slots, span, state),
        jnp.swapaxes(conv_state, 0, 1).reshape(taps, slots, channels),
    )

    own_a, own_b, branch, loops = pl.pallas_call(
        functools.partial(route_kernel, graphs, replicas, slots),
        out_shape=(
            packed,
            packed,
            jax.ShapeDtypeStruct((1,), jnp.int32),
            jax.ShapeDtypeStruct((2,), jnp.int32),
        ),
        in_specs=[smem] * 2 + [vmem] * (replicas + 1),
        out_specs=(vmem, vmem, smem, smem),
        scratch_shapes=[
            VMEM((2, block, channels), F32),
            VMEM((2, win_size, state), F32),
            pltpu.SemaphoreType.DMA((slots,)),
        ],
        compiler_params=pltpu.CompilerParams(vmem_limit_bytes=16 * 2**20),
        name="route",
    )(dst_replica, dst_slot, *others, states, windows)

    def along(first, second):
        def send(rows_a, rows_b):
            out = []
            for value, targets in ((rows_a, first), (rows_b, second)):
                moves = [(s, d) for s, d in enumerate(targets) if s != d]
                out.append(lax.ppermute(value, "replica", moves) if moves else value)
            return tuple(out)

        return send

    branches = tuple(
        jax.make_jaxpr(along(first, second))(own_a, own_b) for _, _, first, second in graphs
    )
    got_a, got_b = lax.cond_p.bind(branch[0], own_a, own_b, branches=branches)
    arrived = (got_a, got_b, own_a, own_b)

    partial, updates, inputs, last_window, order, scale = pl.pallas_call(
        mix_kernel,
        out_shape=(
            jax.ShapeDtypeStruct((2 * slots, columns), BF16),
            jax.ShapeDtypeStruct((2, slots, span), F32),
            jax.ShapeDtypeStruct((2, slots, state), F32),
            jax.ShapeDtypeStruct((slots, channels), F32),
            jax.ShapeDtypeStruct((slots, state), F32),
            jax.ShapeDtypeStruct((slots, heads), F32),
        ),
        in_specs=[smem, smem] + [any_spec] * 4 + [vmem] * len(small) + [any_spec],
        out_specs=(vmem,) * 6,
        scratch_shapes=[
            VMEM((slots, span, state), BF16),
            VMEM((2, win_size, state), BF16),
            VMEM(out_weight.shape, BF16),
            VMEM((5 * slots, span), F32),
            VMEM((2, slots, span), F32),
            VMEM((2, slots, channels), F32),
            VMEM((1, span), F32),
            pltpu.SemaphoreType.DMA((slots,)),
            pltpu.SemaphoreType.DMA((2,)),
            pltpu.SemaphoreType.DMA((8,)),
        ],
        compiler_params=pltpu.CompilerParams(vmem_limit_bytes=52 * 2**20),
        name="mix",
    )(
        loops,
        live,
        *arrived,
        *small,
        out_weight,
    )

    members = lax.axis_size("tensor")
    terms = [partial] + [
        lax.ppermute(partial, "tensor", [(i, i ^ k) for i in range(members)])
        for k in range(1, members)
    ]
    states_out, windows_out = pl.pallas_call(
        state_kernel,
        out_shape=(
            jax.ShapeDtypeStruct((slots, span, state), BF16),
            jax.ShapeDtypeStruct((taps, slots, channels), BF16),
        ),
        in_specs=[smem, smem] + [any_spec] * 4 + [vmem] * 6,
        out_specs=(any_spec, vmem),
        scratch_shapes=[
            VMEM((slots, span, state), BF16),
            VMEM((slots, span, state), BF16),
            pltpu.SemaphoreType.DMA((slots,)),
            pltpu.SemaphoreType.DMA((slots,)),
        ],
        compiler_params=pltpu.CompilerParams(vmem_limit_bytes=52 * 2**20),
        cost_estimate=pl.CostEstimate(
            flops=40 * slots * span * state,
            bytes_accessed=4 * slots * span * state,
            transcendentals=0,
        ),
        name="states",
    )(loops, live, *arrived, updates, inputs, scale, last_window, order, tokens)

    terms = [term.astype(F32) for term in terms]
    while len(terms) > 1:
        terms = [terms[i] + terms[i + 1] for i in range(0, len(terms), 2)]
    mixed = terms[0].astype(BF16).reshape(2, slots, columns)
    conv_after = jnp.swapaxes(windows_out, 0, 1)[:, :, None, :]
    return mixed, states_out.reshape(ssm_state.shape), conv_after


def convolve(window_rows, conv_tokens, conv_weight, conv_bias):
    weight_rows = conv_weight.astype(jnp.float32)
    shift_rows = conv_bias.astype(jnp.float32)
    activations = []
    for step_index in range(conv_tokens.shape[0]):
        stacked = jnp.concatenate([window_rows, conv_tokens[step_index][:, None]], axis=1)
        summed = jnp.sum(stacked.astype(jnp.float32) * weight_rows[None], axis=1) + shift_rows
        activations.append(jax.nn.silu(summed))
        window_rows = stacked[:, 1:]
    return (activations, window_rows)


def advance(
    states_now,
    activations,
    dt_tokens,
    gate_tokens,
    dt_bias,
    a_log,
    skip_gain,
    norm_gain,
    heads_per_group,
):
    decay_rate = -jnp.exp(a_log)
    row_count, head_count, head_width, state_width = states_now.shape
    group_span = heads_per_group * head_width
    normed_list = []
    for step_index in range(len(activations)):
        act_rows = activations[step_index]
        group_count = act_rows.shape[1]
        values = act_rows[..., :group_span].reshape(row_count, head_count, head_width)
        input_map = jnp.repeat(
            act_rows[..., group_span : group_span + state_width], heads_per_group, axis=1
        )
        output_map = jnp.repeat(act_rows[..., group_span + state_width :], heads_per_group, axis=1)
        step_size = jax.nn.softplus(dt_tokens[step_index].astype(jnp.float32) + dt_bias)
        retained = jnp.exp(step_size * decay_rate)
        states_now = (
            retained[:, :, None, None] * states_now
            + (step_size[:, :, None] * values)[:, :, :, None] * input_map[:, :, None, :]
        )
        readout = (
            jnp.einsum("shpn,shn->shp", states_now, output_map, precision=lax.Precision.HIGHEST)
            + skip_gain[None, :, None] * values
        )
        gated_rows = readout.reshape(row_count, head_count * head_width) * jax.nn.silu(
            gate_tokens[step_index].astype(jnp.float32)
        )
        grouped = gated_rows.reshape(row_count, group_count, group_span)
        factor = lax.rsqrt(jnp.mean(grouped * grouped, axis=-1, keepdims=True) + 1e-05)
        normed = (grouped * factor).reshape(row_count, head_count * head_width) * norm_gain.astype(
            jnp.float32
        )
        normed_list.append(normed.astype(jnp.bfloat16))
    return (jnp.stack(normed_list), states_now)


def arrival_rows(received_ids, slot_count):
    wanted = jnp.arange(slot_count, dtype=jnp.int32)[:, None] == received_ids[None, :]
    buffer_index = jnp.arange(received_ids.shape[0], dtype=jnp.int32)
    return jnp.sum(jnp.where(wanted, buffer_index[None, :], 0), axis=1)


def padded(
    ssm_state,
    conv_state,
    dst_replica,
    dst_slot,
    live,
    conv_in,
    gate_in,
    dt_in,
    conv_weight,
    conv_bias,
    dt_bias,
    a_log,
    skip_gain,
    norm_gain,
    out_weight,
):
    replicas = lax.axis_size("replica")
    own_replica = lax.axis_index("replica")
    slot_count = ssm_state.shape[0]
    capacity = max(2, 2 * slot_count // replicas)
    row_index = jnp.arange(slot_count, dtype=jnp.int32)
    same_target = dst_replica[:, None] == dst_replica[None, :]
    earlier_rows = row_index[None, :] < row_index[:, None]
    member = jnp.sum(jnp.where(same_target & earlier_rows, 1, 0), axis=1).astype(jnp.int32)
    position = dst_replica * capacity + member
    buffer_rows = jnp.arange(replicas * capacity, dtype=jnp.int32)
    hit_table = position[None, :] == buffer_rows[:, None]
    picked = jnp.sum(jnp.where(hit_table, row_index[None, :], 0), axis=1)
    filled = jnp.any(hit_table, axis=1)
    send_ids = jnp.where(filled, jnp.take(dst_slot, picked), -1)
    send_windows = jnp.where(
        filled[:, None, None, None],
        jnp.take(conv_state, picked, axis=0),
        jnp.zeros((), conv_state.dtype),
    )
    send_states = jnp.where(
        filled[:, None, None, None],
        jnp.take(ssm_state, picked, axis=0),
        jnp.zeros((), ssm_state.dtype),
    )
    got_states, got_windows, got_ids = (
        lax.all_to_all(send_states, "replica", split_axis=0, concat_axis=0, tiled=True),
        lax.all_to_all(send_windows, "replica", split_axis=0, concat_axis=0, tiled=True),
        lax.all_to_all(send_ids, "replica", split_axis=0, concat_axis=0, tiled=True),
    )
    arrival = arrival_rows(got_ids, slot_count)
    windows_now = jnp.take(got_windows, arrival, axis=0)
    activations, windows_end = convolve(windows_now, conv_in, conv_weight, conv_bias)
    states_now = jnp.take(got_states, arrival, axis=0).astype(jnp.float32)
    normed_all, states_end = advance(
        states_now,
        activations,
        dt_in,
        gate_in,
        dt_bias,
        a_log,
        skip_gain,
        norm_gain,
        HEADS // GROUPS,
    )
    step_count = normed_all.shape[0]
    partial_value = jnp.dot(
        normed_all.reshape(step_count * slot_count, normed_all.shape[2]),
        out_weight,
        preferred_element_type=jnp.float32,
    )
    summed = lax.psum(partial_value, "tensor").astype(jnp.bfloat16)
    live_rows = row_index < live[own_replica]
    mixed = jnp.where(
        live_rows[None, :, None],
        summed.reshape(step_count, slot_count, summed.shape[1]),
        jnp.zeros((), jnp.bfloat16),
    )
    ssm_after = jnp.where(
        live_rows[:, None, None, None], states_end.astype(jnp.bfloat16), jnp.zeros((), jnp.bfloat16)
    )
    conv_after = jnp.where(
        live_rows[:, None, None, None], windows_end, jnp.zeros((), windows_end.dtype)
    )
    return (mixed, ssm_after, conv_after)


def solution(mesh):
    placed = (
        P(("groups", "replica"), "tensor", None, None),
        P(("groups", "replica"), None, "tensor", None),
        P(("groups", "replica")),
        P(("groups", "replica")),
        P("groups"),
        P(None, ("groups", "replica"), "tensor", None),
        P(None, ("groups", "replica"), "tensor"),
        P(None, ("groups", "replica"), "tensor"),
        P(None, "tensor", None),
        P("tensor", None),
        P("tensor"),
        P("tensor"),
        P("tensor"),
        P("tensor"),
        P("tensor", None),
    )
    shards = routed if mesh.shape["replica"] == 4 else padded
    return jax.shard_map(
        shards,
        mesh=mesh,
        in_specs=placed,
        out_specs=(
            P(None, ("groups", "replica"), None),
            P(("groups", "replica"), "tensor", None, None),
            P(("groups", "replica"), None, "tensor", None),
        ),
        check_vma=False,
    )
```
